128 devices in a mesh: dp: 16 (over x, y_hi, core), tensor: 8 (over z, y_lo).
Axes of the slice: x: 4, y: 4 (y_hi: 2, y_lo: 2; y = y_hi * 2 + y_lo), z: 4, core: 2. Of those that a mesh axis runs over, the one named last changes fastest.
Arguments:
- stream: bfloat16 [8192, 4096], P(('dp', 'tensor')), may hold values from -16 to 16
- final_gain: float32 [4096], replicated, may hold values from 0.1 to 1.9
- residual: bfloat16 [8192, 4096], P(('dp', 'tensor')), may hold values from -16 to 16
- ffn_gain: float32 [4096], replicated, may hold values from 0.1 to 1.9
- queries: bfloat16 [4096, 2048], P('dp', 'tensor'), may hold values from -2 to 2
- saved_keys: bfloat16 [8192, 2048], P('dp', 'tensor'), may hold values from -1.75 to 1.75
- saved_values: bfloat16 [8192, 2048], P('dp', 'tensor'), may hold values from -6 to 6
- context_grad: bfloat16 [4096, 2048], P('dp', 'tensor'), may hold values from -24 to 24
- key_weight: bfloat16 [4096, 2048], P('dp', 'tensor'), may hold values from -0.09375 to 0.09375
- value_weight: bfloat16 [4096, 2048], P('dp', 'tensor'), may hold values from -0.09375 to 0.09375
- gate_weight: bfloat16 [4096, 8192], P(None, 'tensor'), may hold values from -0.09375 to 0.09375
- up_weight: bfloat16 [4096, 8192], P(None, 'tensor'), may hold values from -0.09375 to 0.09375
- down_weight: bfloat16 [8192, 4096], P('tensor', 'dp'), may hold values from -0.0625 to 0.0625
Outputs:
- residual_grad: bfloat16 [8192, 4096], P(('dp', 'tensor'))
- query_grad: bfloat16 [4096, 2048], P('dp', 'tensor')
- key_weight_grad: bfloat16 [4096, 2048], P('dp', 'tensor')
- value_weight_grad: bfloat16 [4096, 2048], P('dp', 'tensor')
The draws below stay inside these ranges and needn't reach their ends.
All inputs are finite; a program needn't handle non-finite values.
Results may differ from the reference program's by a relative error of at most 0.03.
Values may be sent and summed in bfloat16 or wider, within the bound.
A program may use at most 192 MiB of HBM per device.

```python
import math
import jax
import jax.numpy as jnp
from jax import lax

D = 4096
HEADS = 8
HEAD_DIM = 256
FF = 8192
ENC_TOK = 512
DEC_TOK = 256
INNER = 2048
ENC_ALL = 8192
DEC_ALL = 4096
N_TENSOR = 8


def rough_scales(key, spread):
    log_spread = math.log(spread)
    row_scale = jnp.exp(-jax.random.uniform(jax.random.fold_in(key, 7), (ENC_ALL, 1), jnp.float32, 0.0, log_spread))
    col_scale = jnp.exp(jax.random.uniform(jax.random.fold_in(key, 8), (1, D), jnp.float32, -0.5 * log_spread, 0.5 * log_spread))
    return row_scale * col_scale


def shared_keys(key):
    base_keys = jax.random.uniform(jax.random.fold_in(key, 101), (ENC_ALL, INNER), jnp.float32, -1.7320508, 1.7320508)
    return base_keys


def draw_stream(key, part):
    key = jax.random.fold_in(key, 21)
    entries = jnp.clip(jax.random.normal(jax.random.fold_in(key, 1), (ENC_ALL, D), jnp.float32), -4.0, 4.0)
    scaled = entries * rough_scales(key, 10.0)
    return scaled.astype(jnp.bfloat16)


def draw_residual(key, part):
    key = jax.random.fold_in(key, 22)
    entries = jnp.clip(jax.random.normal(jax.random.fold_in(key, 1), (ENC_ALL, D), jnp.float32), -4.0, 4.0)
    scaled = entries * rough_scales(key, 10.0)
    return scaled.astype(jnp.bfloat16)


def draw_saved_keys(key, part):
    base_keys = shared_keys(key)
    return base_keys.astype(jnp.bfloat16)


def draw_queries(key, part):
    key = jax.random.fold_in(key, 5)
    query_rows = jnp.clip(jax.random.normal(key, (DEC_ALL, INNER), jnp.float32), -4.0, 4.0) * 0.0625
    return query_rows.astype(jnp.bfloat16)


def block_levels(own_key, shape, pieces, smallest, high):
    loudness, own = 1.0, jax.random.fold_in(own_key, 6)
    for axis_at, parts in pieces:
        draws = jnp.exp(jax.random.uniform(jax.random.fold_in(own, axis_at), (parts,), jnp.float32, smallest / len(pieces), high / len(pieces)))
        loudness = loudness * jnp.repeat(draws, shape[axis_at] // parts).reshape([-1 if axis == axis_at else 1 for axis in range(len(shape))])
    return loudness


def centred(key, dims, scale, bound, cuts=(), held_as=jnp.bfloat16):
    values = jax.random.normal(key, dims, jnp.float32) * scale
    if len(cuts) > 0:
        values = block_levels(key, dims, cuts, -0.22, 0.18) * values
    return jnp.clip(values, min=-bound, max=bound).astype(held_as)


def setup_inputs(seed: int = 0) -> dict:
    keys = jax.random.split(jax.random.key(seed), 14)
    return {
        "stream": draw_stream(jax.random.fold_in(keys[13], 71), 0),
        "final_gain": jnp.clip(1.0 + 0.18 * jax.random.normal(keys[1], (D,), jnp.float32), 0.1, 1.9),
        "residual": draw_residual(jax.random.fold_in(keys[13], 71), 0),
        "ffn_gain": jnp.clip(1.0 + 0.18 * jax.random.normal(keys[3], (D,), jnp.float32), 0.1, 1.9),
        "queries": draw_queries(jax.random.fold_in(keys[13], 71), 0),
        "saved_keys": draw_saved_keys(jax.random.fold_in(keys[13], 71), 0),
        "saved_values": centred(keys[6], (ENC_ALL, INNER), 1.0, 6.0, ((0, 16), (1, 8))),
        "context_grad": centred(keys[7], (DEC_ALL, INNER), 4.0, 24.0, ((0, 16), (1, 8))),
        "key_weight": centred(keys[8], (D, INNER), D ** -0.5, 0.09375, ((0, 16), (1, 8))),
        "value_weight": centred(keys[9], (D, INNER), D ** -0.5, 0.09375, ((0, 16), (1, 8))),
        "gate_weight": centred(keys[10], (D, FF), D ** -0.5, 0.09375, ((1, 8),)),
        "up_weight": centred(keys[11], (D, FF), D ** -0.5, 0.09375, ((1, 8),)),
        "down_weight": centred(keys[12], (FF, D), FF ** -0.5, 0.0625, ((0, 8), (1, 16))),
    }


def rms_scale(values_wide):
    return lax.rsqrt(lax.optimization_barrier(jnp.mean(values_wide * values_wide, axis=-1, keepdims=True)) + 1e-06)

def norm_back(grad_in, values_wide, scale, gain):
    scaled = grad_in * gain
    return scale * scaled - values_wide * (scale * scale * scale) * lax.optimization_barrier(jnp.mean(scaled * values_wide, axis=-1, keepdims=True))

def reference(stream, final_gain, residual, ffn_gain, queries, saved_keys, saved_values, context_grad, key_weight, value_weight, gate_weight, up_weight, down_weight):
    groups = ENC_ALL // ENC_TOK
    stream_wide = stream.astype(jnp.float32)
    enc_scale = rms_scale(stream_wide)
    enc_out = (stream_wide * enc_scale * final_gain).astype(jnp.bfloat16)
    query_heads = queries.astype(jnp.float32).reshape(groups, DEC_TOK, HEADS, HEAD_DIM)
    key_heads = saved_keys.astype(jnp.float32).reshape(groups, ENC_TOK, HEADS, HEAD_DIM)
    value_heads = saved_values.astype(jnp.float32).reshape(groups, ENC_TOK, HEADS, HEAD_DIM)
    out_grad = context_grad.astype(jnp.float32).reshape(groups, DEC_TOK, HEADS, HEAD_DIM)
    scores = jnp.einsum('gqhd,gkhd->ghqk', query_heads, key_heads)
    attn_probs = jax.nn.softmax(scores, axis=-1)
    probs_low = lax.optimization_barrier(attn_probs.astype(jnp.bfloat16)).astype(jnp.float32)
    prob_grad = jnp.einsum('gqhd,gkhd->ghqk', out_grad, value_heads)
    row_delta = lax.optimization_barrier(jnp.sum(attn_probs * prob_grad, axis=-1, keepdims=True))
    score_grad = lax.optimization_barrier((attn_probs * (prob_grad - row_delta)).astype(jnp.bfloat16)).astype(jnp.float32)
    value_grad = jnp.einsum('ghqk,gqhd->gkhd', probs_low, out_grad).astype(jnp.bfloat16).reshape(ENC_ALL, INNER)
    key_grad = jnp.einsum('ghqk,gqhd->gkhd', score_grad, query_heads).astype(jnp.bfloat16).reshape(ENC_ALL, INNER)
    query_grad = jnp.einsum('ghqk,gkhd->gqhd', score_grad, key_heads).astype(jnp.bfloat16).reshape(DEC_ALL, INNER)
    key_weight_grad = jnp.dot(enc_out.T, key_grad, preferred_element_type=jnp.float32).astype(jnp.bfloat16)
    value_weight_grad = jnp.dot(enc_out.T, value_grad, preferred_element_type=jnp.float32).astype(jnp.bfloat16)
    block_width = INNER // N_TENSOR
    enc_grad = jnp.zeros((ENC_ALL, D), jnp.float32)
    for block in range(N_TENSOR):
        low = block * block_width
        high = low + block_width
        block_sum = jnp.dot(key_grad[:, low:high], key_weight[:, low:high].T, preferred_element_type=jnp.float32)
        block_sum = block_sum + jnp.dot(value_grad[:, low:high], value_weight[:, low:high].T, preferred_element_type=jnp.float32)
        enc_grad = enc_grad + lax.optimization_barrier(block_sum.astype(jnp.bfloat16)).astype(jnp.float32)
    stream_grad = norm_back(enc_grad, stream_wide, enc_scale, final_gain)
    ffn_grad = stream_grad.astype(jnp.bfloat16)
    resid_wide = residual.astype(jnp.float32)
    res_scale = rms_scale(resid_wide)
    ffn_in = (resid_wide * res_scale * ffn_gain).astype(jnp.bfloat16)
    gate_pre = jnp.dot(ffn_in, gate_weight, preferred_element_type=jnp.float32)
    up_pre = jnp.dot(ffn_in, up_weight, preferred_element_type=jnp.float32)
    hidden_grad = jnp.dot(ffn_grad, down_weight.T, preferred_element_type=jnp.float32)
    gate_sig = jax.nn.sigmoid(gate_pre)
    gate_grad = (hidden_grad * up_pre * gate_sig * (1.0 + gate_pre * (1.0 - gate_sig))).astype(jnp.bfloat16)
    up_grad = (hidden_grad * gate_pre * gate_sig).astype(jnp.bfloat16)
    hidden_width = FF // N_TENSOR
    in_grad = jnp.zeros((ENC_ALL, D), jnp.float32)
    for block in range(N_TENSOR):
        low = block * hidden_width
        high = low + hidden_width
        block_sum = jnp.dot(gate_grad[:, low:high], gate_weight[:, low:high].T, preferred_element_type=jnp.float32)
        block_sum = block_sum + jnp.dot(up_grad[:, low:high], up_weight[:, low:high].T, preferred_element_type=jnp.float32)
        in_grad = in_grad + lax.optimization_barrier(block_sum.astype(jnp.bfloat16)).astype(jnp.float32)
    residual_grad = (stream_grad + norm_back(in_grad, resid_wide, res_scale, ffn_gain)).astype(jnp.bfloat16)
    return (residual_grad, query_grad, key_weight_grad, value_weight_grad)
```

```python
import jax
import jax.numpy as jnp
from jax import lax
from jax.experimental import pallas as pl
from jax.experimental.pallas import tpu as pltpu
from jax.sharding import PartitionSpec as P

BF = jnp.bfloat16
F32 = jnp.float32
D, TOK, OWN, FFL, HD, Q = 4096, 512, 64, 1024, 256, 256
NCH, CW = 8, 512
WCH, WR = 4, 128

NN = (((1,), (0,)), ((), ()))
NT = (((1,), (1,)), ((), ()))
TN = (((0,), (0,)), ((), ()))


def dot(a, b, dims=NN):
    return lax.dot_general(a, b, dims, preferred_element_type=F32)


class Place:
    def __init__(self):
        dp, tn = lax.axis_index("dp"), lax.axis_index("tensor")
        self.dp, self.tn = dp, tn
        self.x, self.h, self.c = dp // 4, (dp // 2) % 2, dp % 2
        self.z, self.l = tn // 2, tn % 2
        self.xu, self.xd, self.x2 = (self.x + 1) % 4, (self.x + 3) % 4, (self.x + 2) % 4
        self.zu, self.zd, self.z2 = (self.z + 1) % 4, (self.z + 3) % 4, (self.z + 2) % 4


def dp_of(x, h, c):
    return (x * 2 + h) * 2 + c


def tn_of(z, l):
    return z * 2 + l


def remote(src, dst, ss, rs, dev):
    return pltpu.make_async_remote_copy(
        src_ref=src, dst_ref=dst, send_sem=ss, recv_sem=rs, device_id=dev,
        device_id_type=pl.DeviceIdType.MESH,
    )


class TensorGather:
    def __init__(self, p, buf, ss, rs):
        z, l, zu, zd, z2, m = p.z, p.l, p.zu, p.zd, p.z2, 1 - p.l
        up, dn, pair = {"tensor": tn_of(zu, l)}, {"tensor": tn_of(zd, l)}, {"tensor": tn_of(z, m)}
        self.buf, self.ss, self.rs = buf, ss, rs
        self.t = [
            ((z, l), (z, m), 0, OWN, pair),
            ((z, l), (zd, l), 0, OWN, up),
            ((z, l), (zu, l), 0, OWN, dn),
            ((z, m), (zd, m), 0, OWN, up),
            ((z, m), (zu, m), 0, OWN, dn),
            ((zd, l), (z2, l), 0, OWN // 2, up),
            ((zu, l), (z2, l), OWN // 2, OWN // 2, dn),
            ((zd, m), (z2, m), 0, OWN // 2, up),
            ((zu, m), (z2, m), OWN // 2, OWN // 2, dn),
        ]

    def _rows(self, shard, first, n):
        return self.buf.at[pl.ds(pl.multiple_of(tn_of(*shard) * OWN + first, 32), n)]

    def _copy(self, i, received):
        sent, got, first, n, to = self.t[i]
        ref = self._rows(got if received else sent, first, n)
        return remote(ref, ref, self.ss.at[i], self.rs.at[i], to)

    def send(self, *idx):
        for i in idx:
            self._copy(i, False).start()

    def recv(self, *idx):
        for i in idx:
            self._copy(i, True).wait_recv()

    def s0(self):
        self.send(0, 1, 2)

    def s1(self):
        self.recv(0)
        self.send(3, 4)

    def s2(self):
        self.recv(1)
        self.send(5)
        self.recv(2)
        self.send(6)

    def s3(self):
        self.recv(3)
        self.send(7)
        self.recv(4)
        self.send(8)

    def s4(self):
        self.recv(5, 6, 7, 8)

    def drain(self):
        for i in range(9):
            self._copy(i, False).wait_send()


class DpGather:
    def __init__(self, p, buf, ss, rs, rows):
        x, h, c, xu, xd, x2, o, g = p.x, p.h, p.c, p.xu, p.xd, p.x2, 1 - p.h, 1 - p.c
        up, dn = {"dp": dp_of(xu, h, c)}, {"dp": dp_of(xd, h, c)}
        pair, core = {"dp": dp_of(x, o, c)}, {"dp": dp_of(x, h, g)}
        self.buf, self.ss, self.rs = buf, ss, rs
        r, hf = rows, rows // 2
        self.t = [
            ((x, h, c), (x, h, g), 0, r, core),
            ((x, h, c), (x, o, c), 0, r, pair),
            ((x, h, c), (xd, h, c), 0, r, up),
            ((x, h, c), (xu, h, c), 0, r, dn),
            ((x, o, c), (xd, o, c), 0, r, up),
            ((x, o, c), (xu, o, c), 0, r, dn),
            ((xd, h, c), (x2, h, c), 0, hf, up),
            ((xu, h, c), (x2, h, c), hf, hf, dn),
            ((xd, o, c), (x2, o, c), 0, hf, up),
            ((xu, o, c), (x2, o, c), hf, hf, dn),
            ((x, o, c), (x, o, g), 0, r, core),
            ((xd, h, c), (xd, h, g), 0, r, core),
            ((xu, h, c), (xu, h, g), 0, r, core),
            ((xd, o, c), (xd, o, g), 0, r, core),
            ((xu, o, c), (xu, o, g), 0, r, core),
            ((x2, h, c), (x2, h, g), 0, r, core),
            ((x2, o, c), (x2, o, g), 0, r, core),
        ]

    def _copy(self, i, received, src=None):
        sent, got, first, n, to = self.t[i]
        sx, sh, sc = got if received else sent
        ref = self.buf.at[sc, sx * 2 + sh, pl.ds(first, n)]
        return remote(ref if src is None else src, ref, self.ss.at[i], self.rs.at[i], to)

    def send(self, *idx, src=None):
        for i in idx:
            self._copy(i, False, src).start()

    def recv(self, *idx):
        for i in idx:
            self._copy(i, True).wait_recv()

    def s0(self, src=None):
        self.send(1, 2, 3, 0, src=src)

    def step(self, k):
        if k == 0:
            self.recv(0)
        elif k < 6:
            self.recv(k)
            if k == 1:
                self.send(4, 5, 10)
            else:
                self.send(k + 4, k + 9)
            self.recv(k + 9)
        elif k == 6:
            self.recv(6, 7)
            self.send(15)
            self.recv(15)
        else:
            self.recv(8, 9)
            self.send(16)
            self.recv(16)

    def drain(self):
        for i in range(17):
            self._copy(i, False).wait_send()


class RingReduce:
    def __init__(self, part, far, near, ysend, yrecv, ss, rs, ring, pair, up, dn, mate):
        self.part, self.far, self.near, self.ysend, self.yrecv = part, far, near, ysend, yrecv
        self.ss, self.rs = ss, rs
        self.r, self.ru, self.rd, self.r2 = ring
        self.l, self.m = pair, 1 - pair
        self.up, self.dn, self.mate = up, dn, mate

    def _copy(self, i, k):
        p = self.part(k)
        src, dst, to = [
            (lambda: p.at[self.r2 * 2], lambda: self.far.at[k, 0], self.up),
            (lambda: p.at[self.r2 * 2 + 1], lambda: self.far.at[k, 1], self.dn),
            (lambda: p.at[self.ru * 2 + 1], lambda: self.near.at[k, 1], self.up),
            (lambda: p.at[self.rd * 2], lambda: self.near.at[k, 2], self.dn),
            (lambda: p.at[self.ru * 2], lambda: self.near.at[k, 0], self.up),
            (lambda: p.at[self.rd * 2 + 1], lambda: self.near.at[k, 3], self.dn),
            (lambda: self.ysend.at[k], lambda: self.yrecv.at[k], self.mate),
        ][i]
        return remote(src(), dst(), self.ss.at[k, i], self.rs.at[k, i], to)

    def stage1(self, k):
        for i in range(4):
            self._copy(i, k).start()

    def stage2(self, k):
        p = self.part(k)
        for i, blk in ((0, self.ru * 2), (1, self.rd * 2 + 1)):
            self._copy(i, k).wait_recv()
            p[blk] = (p[blk].astype(F32) + self.far[k, i].astype(F32)).astype(BF)
            self._copy(4 + i, k).start()

    def stage3(self, k):
        for i in (2, 3, 4, 5):
            self._copy(i, k).wait_recv()
        p = self.part(k)

        def total(pair):
            return (
                p[self.r * 2 + pair].astype(F32)
                + self.near[k, pair].astype(F32)
                + self.near[k, 2 + pair].astype(F32)
            )

        self.ysend[k] = total(self.m).astype(BF)
        self._copy(6, k).start()
        return total(self.l)

    def stage4(self, k):
        self._copy(6, k).wait_recv()
        return self.yrecv[k].astype(F32)

    def drain(self, n):
        def body(k, _):
            for i in range(7):
                self._copy(i, k).wait_send()
            return 0

        lax.fori_loop(0, n, body, 0)


def kernel(
    stream, final_gain, residual, ffn_gain, queries, keys, values, ctx, key_w, value_w,
    gate_hbm, up_hbm, down_hbm,
    out_ref, qg_ref, kwg_ref, vwg_ref, down_all,
    res_g, str_g, ffn_g, kvw, gate_v, up_v, down_v, part, far, near, ysend, yrecv,
    coef_a, coef_b, ggrad, ugrad, acc, sgrad, kvg, kvg_t,
    crecv, wfar, wnear, wysend, wyrecv, wacc,
    res_ss, res_rs, str_ss, str_rs, ffn_ss, ffn_rs, kv_ss, kv_rs, dn_ss, dn_rs,
    er_ss, er_rs, ir_ss, ir_rs, wr_ss, wr_rs, cs_ss, cs_rs, loc, dsem,
):
    p = Place()
    MESH = pl.DeviceIdType.MESH
    z_up, z_dn = {"tensor": tn_of(p.zu, p.l)}, {"tensor": tn_of(p.zd, p.l)}
    mate = {"tensor": tn_of(p.z, 1 - p.l)}
    x_up, x_dn = {"dp": dp_of(p.xu, p.h, p.c)}, {"dp": dp_of(p.xd, p.h, p.c)}
    h_mate, core = {"dp": dp_of(p.x, 1 - p.h, p.c)}, {"dp": dp_of(p.x, p.h, 1 - p.c)}

    barrier = pltpu.get_barrier_semaphore()
    for dev in (z_up, z_dn, mate, x_up, x_dn, h_mate, core):
        pl.semaphore_signal(barrier, inc=1, device_id=dev, device_id_type=MESH)

    own_chip = p.x * 2 + p.h
    gate_load = pltpu.make_async_copy(gate_hbm, gate_v, loc.at[0])
    up_load = pltpu.make_async_copy(up_hbm, up_v, loc.at[1])
    down_own = pltpu.make_async_copy(down_hbm, down_all.at[p.c, own_chip], loc.at[2])
    down_own.start()
    gate_load.start()
    up_load.start()

    kvw[p.c, own_chip, 0:HD, :] = key_w[...]
    kvw[p.c, own_chip, HD : 2 * HD, :] = value_w[...]
    own = pl.multiple_of(p.tn * OWN, OWN)

    def normed(src, gain, dst):
        def body(i, _):
            r = pl.multiple_of(i * 16, 16)
            v = src[pl.ds(r, 16), :].astype(F32)
            s = lax.rsqrt(jnp.mean(v * v, axis=-1, keepdims=True) + 1e-06)
            dst[pl.ds(pl.multiple_of(own + r, 16), 16), :] = (v * s * gain[...]).astype(BF)
            return 0

        lax.fori_loop(0, OWN // 16, body, 0)

    kv = DpGather(p, kvw, kv_ss, kv_rs, 2 * HD)
    down = DpGather(p, down_all, dn_ss, dn_rs, FFL)
    res = TensorGather(p, res_g, res_ss, res_rs)
    stm = TensorGather(p, str_g, str_ss, str_rs)
    ffn = TensorGather(p, ffn_g, ffn_ss, ffn_rs)

    pl.semaphore_wait(barrier, 7)
    kv.s0()
    normed(residual, ffn_gain, res_g)
    res.s0()
    normed(stream, final_gain, str_g)
    stm.s0()

    s_t = dot(keys[...], queries[...], NT)
    e_t = jnp.exp(s_t - jnp.max(s_t, axis=0, keepdims=True))
    probs = e_t / jnp.sum(e_t, axis=0, keepdims=True)
    pg = dot(values[...], ctx[...], NT)
    delta = jnp.sum(probs * pg, axis=0, keepdims=True)
    sg = (probs * (pg - delta)).astype(BF)
    vgrad = dot(probs.astype(BF), ctx[...])
    kgrad = dot(sg, queries[...])
    kvg[:, 0:HD] = kgrad.astype(BF)
    kvg[:, HD : 2 * HD] = vgrad.astype(BF)
    kvg_t[0:HD, :] = kgrad.T.astype(BF)
    kvg_t[HD : 2 * HD, :] = vgrad.T.astype(BF)
    qg_ref[...] = dot(sg, keys[...], TN).astype(BF)

    ring_z = (p.z, p.zu, p.zd, p.z2)
    ring_x = (p.x, p.xu, p.xd, p.x2)
    enc_rs = RingReduce(
        lambda k: part.at[k], far, near, ysend, yrecv, er_ss, er_rs, ring_z, p.l, z_up, z_dn, mate
    )
    in_rs = RingReduce(
        lambda k: part.at[k], far, near, ysend, yrecv, ir_ss, ir_rs, ring_z, p.l, z_up, z_dn, mate
    )
    w_rs = RingReduce(
        lambda k: kvw.at[p.c, :, pl.ds(pl.multiple_of(k * WR, WR), WR), :],
        wfar, wnear, wysend, wyrecv, wr_ss, wr_rs, ring_x, p.h, x_up, x_dn, h_mate,
    )

    def chunk_of(k):
        if isinstance(k, int):
            return [
                p.x * 2 + p.h, p.x * 2 + 1 - p.h, p.xd * 2 + p.h, p.xu * 2 + p.h,
                p.xd * 2 + 1 - p.h, p.xu * 2 + 1 - p.h, p.x2 * 2 + p.h, p.x2 * 2 + 1 - p.h,
            ][k]
        raise TypeError

    def enc_compute(k):
        chip = chunk_of(k)
        for cc in range(2):
            blk = dot(kvg[:, 0:HD], kvw[cc, chip, 0:HD, :], NT)
            blk = blk + dot(kvg[:, HD : 2 * HD], kvw[cc, chip, HD : 2 * HD, :], NT)
            part[k, :, :, cc * HD : (cc + 1) * HD] = blk.astype(BF).reshape(8, OWN, HD)

    services = {
        1: [res.s1],
        2: [res.s2],
        4: [stm.s1],
        5: [res.s3],
        6: [stm.s2],
        8: [stm.s3],
    }
    for k in range(NCH + 3):
        if k < NCH:
            kv.step(k)
            enc_compute(k)
            enc_rs.stage1(k)
        for service in services.get(k, []):
            service()
        if k == 4:
            down_own.wait()
            down.s0()
        if 0 <= k - 1 < NCH:
            enc_rs.stage2(k - 1)
        if 0 <= k - 2 < NCH:
            acc[k - 2] = enc_rs.stage3(k - 2)
        if 0 <= k - 3 < NCH:
            acc[k - 3] = acc[k - 3] + enc_rs.stage4(k - 3)

    def cols(k):
        start = chunk_of(k) * CW
        return pl.ds(pl.multiple_of(start, CW), CW)

    sq = jnp.zeros((OWN, 1), F32)
    ip = jnp.zeros((OWN, 1), F32)
    for k in range(NCH):
        v = stream[:, cols(k)].astype(F32)
        sq = sq + jnp.sum(v * v, axis=-1, keepdims=True)
        ip = ip + jnp.sum(acc[k] * final_gain[:, cols(k)] * v, axis=-1, keepdims=True)
    scale = lax.rsqrt(sq * (1.0 / D) + 1e-06)
    mix = scale * scale * scale * (ip * (1.0 / D))
    for k in range(NCH):
        v = stream[:, cols(k)].astype(F32)
        grad = scale * (acc[k] * final_gain[:, cols(k)]) - v * mix
        sgrad[:, cols(k)] = grad
        ffn_g[pl.ds(own, OWN), cols(k)] = grad.astype(BF)
    ffn.s0()

    gate_load.wait()
    up_load.wait()
    down.step(0)
    down.step(1)
    res.s4()

    def gate_tile(j):
        c0 = pl.ds(pl.multiple_of(j * HD, HD), HD)
        gate = dot(res_g[...], gate_v[:, c0])
        up = dot(res_g[...], up_v[:, c0])
        sig = 1.0 / (1.0 + jnp.exp(-gate))
        coef_a[:, c0] = (up * sig * (1.0 + gate * (1.0 - sig))).astype(BF)
        coef_b[:, c0] = (gate * sig).astype(BF)

    def gate_tiles(lo, hi):
        lax.fori_loop(lo, hi, lambda j, _: (gate_tile(j), 0)[1], 0)

    gate_tiles(0, 2)
    down.step(2)
    down.step(3)
    ffn.s1()
    gate_tiles(2, 4)
    down.step(4)
    down.step(5)
    ffn.s2()
    stm.s4()
    kv.drain()

    def w_tile(chip, _):
        for cc in range(2):
            c0 = pl.ds(pl.multiple_of((chip * 2 + cc) * HD, HD), HD)
            kvw[cc, chip] = dot(kvg_t[...], str_g[:, c0]).astype(BF)
        return 0

    lax.fori_loop(0, 8, w_tile, 0)
    down.step(6)
    down.step(7)

    def down_load(j):
        s = j % 2
        return pltpu.make_async_copy(
            down_all.at[:, :, pl.ds(pl.multiple_of(j * HD, HD), HD), :], down_v.at[s], dsem.at[s]
        )

    down_load(0).start()
    ffn.s3()

    def core_copy(k):
        rows = pl.ds(pl.multiple_of(k * WR, WR), WR)
        return remote(
            kvw.at[1 - p.c, :, rows, :], crecv.at[k], cs_ss.at[k], cs_rs.at[k], core
        )

    for k in range(WCH):
        core_copy(k).start()
    enc_rs.drain(NCH)
    ffn.s4()

    def hidden_tile(j, _):
        @pl.when(j < 3)
        def _():
            down_load(j + 1).start()

        down_load(j).wait()
        s = j % 2
        hid = jnp.zeros((TOK, HD), F32)
        for i in range(16):
            hid = hid + dot(ffn_g[:, i * HD : (i + 1) * HD], down_v[s, i % 2, i // 2], NT)
        c0 = pl.ds(pl.multiple_of(j * HD, HD), HD)
        ggrad[:, c0] = (hid * coef_a[:, c0].astype(F32)).astype(BF)
        ugrad[:, c0] = (hid * coef_b[:, c0].astype(F32)).astype(BF)
        return 0

    lax.fori_loop(0, 4, hidden_tile, 0)

    def in_step(k, _):
        @pl.when(k < NCH)
        def _():
            rows = pl.ds(pl.multiple_of(k * CW, CW), CW)
            blk = dot(ggrad[...], gate_v[rows, :], NT) + dot(ugrad[...], up_v[rows, :], NT)
            part[k] = blk.astype(BF).reshape(8, OWN, CW)
            in_rs.stage1(k)

        @pl.when(k < WCH)
        def _():
            core_copy(k).wait_recv()
            mine = w_rs.part(k)
            mine[...] = (mine[...].astype(F32) + crecv[k].astype(F32)).astype(BF)
            w_rs.stage1(k)

        @pl.when((k >= 1) & (k < NCH + 1))
        def _():
            in_rs.stage2(k - 1)

        @pl.when((k >= 1) & (k < WCH + 1))
        def _():
            w_rs.stage2(k - 1)

        @pl.when((k >= 2) & (k < NCH + 2))
        def _():
            acc[k - 2] = in_rs.stage3(k - 2)

        @pl.when((k >= 2) & (k < WCH + 2))
        def _():
            wacc[k - 2] = w_rs.stage3(k - 2)

        @pl.when(k >= 3)
        def _():
            acc[k - 3] = acc[k - 3] + in_rs.stage4(k - 3)

        @pl.when((k >= 3) & (k < WCH + 3))
        def _():
            wacc[k - 3] = wacc[k - 3] + w_rs.stage4(k - 3)

        return 0

    lax.fori_loop(0, NCH + 3, in_step, 0)

    for half in range(2):
        kwg_ref[:, half * WR : (half + 1) * WR] = wacc[half].T.astype(BF)
        vwg_ref[:, half * WR : (half + 1) * WR] = wacc[2 + half].T.astype(BF)

    sq = jnp.zeros((OWN, 1), F32)
    ip = jnp.zeros((OWN, 1), F32)
    for k in range(NCH):
        c0 = slice(k * CW, (k + 1) * CW)
        v = residual[:, c0].astype(F32)
        sq = sq + jnp.sum(v * v, axis=-1, keepdims=True)
        ip = ip + jnp.sum(acc[k] * ffn_gain[:, c0] * v, axis=-1, keepdims=True)
    scale = lax.rsqrt(sq * (1.0 / D) + 1e-06)
    mix = scale * scale * scale * (ip * (1.0 / D))
    for k in range(NCH):
        c0 = slice(k * CW, (k + 1) * CW)
        v = residual[:, c0].astype(F32)
        out_ref[:, c0] = (
            sgrad[:, c0] + scale * (acc[k] * ffn_gain[:, c0]) - v * mix
        ).astype(BF)

    for g in (res, stm, ffn, down):
        g.drain()
    in_rs.drain(NCH)
    w_rs.drain(WCH)
    for k in range(WCH):
        core_copy(k).wait_send()


def local(
    stream, final_gain, residual, ffn_gain, queries, saved_keys, saved_values, context_grad,
    key_weight, value_weight, gate_weight, up_weight, down_weight,
):
    vm = pl.BlockSpec(memory_space=pltpu.VMEM)
    hbm = pl.BlockSpec(memory_space=pl.ANY)
    dma = pltpu.SemaphoreType.DMA
    sds = jax.ShapeDtypeStruct
    v = pltpu.VMEM
    outs = pl.pallas_call(
        kernel,
        out_shape=(
            sds((OWN, D), BF), sds((Q, HD), BF), sds((HD, HD), BF), sds((HD, HD), BF),
            sds((2, 8, FFL, HD), BF),
        ),
        in_specs=[vm] * 10 + [hbm] * 3,
        out_specs=(vm, vm, vm, vm, hbm),
        scratch_shapes=[
            v((TOK, D), BF), v((TOK, D), BF), v((TOK, D), BF),
            v((2, 8, 2 * HD, HD), BF),
            v((D, FFL), BF), v((D, FFL), BF),
            v((2, 2, 8, HD, HD), BF),
            v((NCH, 8, OWN, CW), BF),
            v((NCH, 2, OWN, CW), BF), v((NCH, 4, OWN, CW), BF),
            v((NCH, OWN, CW), BF), v((NCH, OWN, CW), BF),
            v((TOK, FFL), BF), v((TOK, FFL), BF), v((TOK, FFL), BF), v((TOK, FFL), BF),
            v((NCH, OWN, CW), F32), v((OWN, D), F32),
            v((TOK, 2 * HD), BF), v((2 * HD, TOK), BF),
            v((WCH, 8, WR, HD), BF),
            v((WCH, 2, WR, HD), BF), v((WCH, 4, WR, HD), BF),
            v((WCH, WR, HD), BF), v((WCH, WR, HD), BF), v((WCH, WR, HD), F32),
            dma((9,)), dma((9,)), dma((9,)), dma((9,)), dma((9,)), dma((9,)),
            dma((17,)), dma((17,)), dma((17,)), dma((17,)),
            dma((NCH, 7)), dma((NCH, 7)), dma((NCH, 7)), dma((NCH, 7)),
            dma((WCH, 7)), dma((WCH, 7)), dma((WCH,)), dma((WCH,)),
            dma((3,)), dma((2,)),
        ],
        compiler_params=pltpu.CompilerParams(
            collective_id=0, has_side_effects=True, vmem_limit_bytes=64 * 1024 * 1024
        ),
        name="cross_ffn_backward",
    )(
        stream, final_gain.reshape(1, D), residual, ffn_gain.reshape(1, D), queries, saved_keys,
        saved_values, context_grad, key_weight, value_weight, gate_weight, up_weight, down_weight,
    )
    return outs[:4]


def solution(mesh):
    return jax.shard_map(
        local,
        mesh=mesh,
        in_specs=(
            P(("dp", "tensor"), None), P(), P(("dp", "tensor"), None), P(),
            P("dp", "tensor"), P("dp", "tensor"), P("dp", "tensor"), P("dp", "tensor"),
            P("dp", "tensor"), P("dp", "tensor"), P(None, "tensor"), P(None, "tensor"),
            P("tensor", "dp"),
        ),
        out_specs=(
            P(("dp", "tensor"), None), P("dp", "tensor"), P("dp", "tensor"), P("dp", "tensor"),
        ),
        check_vma=False,
    )
```

```python
import jax
import jax.numpy as jnp
from jax import lax
from jax.experimental import pallas as pl
from jax.experimental.pallas import tpu as pltpu
from jax.sharding import PartitionSpec as P

BF = jnp.bfloat16
F32 = jnp.float32
D, TOK, OWN, FFL, HD, Q = 4096, 512, 64, 1024, 256, 256
NCH, CW = 8, 512
WCH, WR = 4, 128
W0 = 4

NN = (((1,), (0,)), ((), ()))
NT = (((1,), (1,)), ((), ()))
TN = (((0,), (0,)), ((), ()))


def dot(a, b, dims=NN):
    return lax.dot_general(a, b, dims, preferred_element_type=F32)


class Place:
    def __init__(self):
        dp, tn = lax.axis_index("dp"), lax.axis_index("tensor")
        self.dp, self.tn = dp, tn
        self.x, self.h, self.c = dp // 4, (dp // 2) % 2, dp % 2
        self.z, self.l = tn // 2, tn % 2
        self.xu, self.xd, self.x2 = (self.x + 1) % 4, (self.x + 3) % 4, (self.x + 2) % 4
        self.zu, self.zd, self.z2 = (self.z + 1) % 4, (self.z + 3) % 4, (self.z + 2) % 4


def dp_of(x, h, c):
    return (x * 2 + h) * 2 + c


def tn_of(z, l):
    return z * 2 + l


def remote(src, dst, ss, rs, dev):
    return pltpu.make_async_remote_copy(
        src_ref=src, dst_ref=dst, send_sem=ss, recv_sem=rs, device_id=dev,
        device_id_type=pl.DeviceIdType.MESH,
    )


class TensorGather:
    def __init__(self, p, buf, ss, rs):
        z, l, zu, zd, z2, m = p.z, p.l, p.zu, p.zd, p.z2, 1 - p.l
        up, dn, pair = {"tensor": tn_of(zu, l)}, {"tensor": tn_of(zd, l)}, {"tensor": tn_of(z, m)}
        self.buf, self.ss, self.rs = buf, ss, rs
        self.t = [
            ((z, l), (z, m), 0, OWN, pair),
            ((z, l), (zd, l), 0, OWN, up),
            ((z, l), (zu, l), 0, OWN, dn),
            ((z, m), (zd, m), 0, OWN, up),
            ((z, m), (zu, m), 0, OWN, dn),
            ((zd, l), (z2, l), 0, OWN // 2, up),
            ((zu, l), (z2, l), OWN // 2, OWN // 2, dn),
            ((zd, m), (z2, m), 0, OWN // 2, up),
            ((zu, m), (z2, m), OWN // 2, OWN // 2, dn),
        ]

    def _rows(self, shard, first, n):
        return self.buf.at[pl.ds(pl.multiple_of(tn_of(*shard) * OWN + first, 32), n)]

    def _copy(self, i, received):
        sent, got, first, n, to = self.t[i]
        ref = self._rows(got if received else sent, first, n)
        return remote(ref, ref, self.ss.at[i], self.rs.at[i], to)

    def send(self, *idx):
        for i in idx:
            self._copy(i, False).start()

    def recv(self, *idx):
        for i in idx:
            self._copy(i, True).wait_recv()

    def s0(self):
        self.send(0, 1, 2)

    def s1(self):
        self.recv(0)
        self.send(3, 4)

    def s2(self):
        self.recv(1)
        self.send(5)
        self.recv(2)
        self.send(6)

    def s3(self):
        self.recv(3)
        self.send(7)
        self.recv(4)
        self.send(8)

    def s4(self):
        self.recv(5, 6, 7, 8)

    def drain(self):
        for i in range(9):
            self._copy(i, False).wait_send()


class ColumnGather:
    def __init__(self, p, buf, ss, rs, up, dn, mate_a, mate_b):
        z, zu, zd, z2 = p.z, p.zu, p.zd, p.z2
        self.buf, self.ss, self.rs = buf, ss, rs
        a, b = (4, mate_a), (6, mate_b)
        self.t = [
            (z, 0, zd, up), (z, 1, zu, dn), (z, 1, zd, up), (z, 0, zu, dn),
            (z, 0, z, a), (z, 1, z, b),
            (zd, 0, z2, up), (zd, 0, zd, a),
            (zu, 1, z2, dn), (zu, 1, zu, b),
            (zd, 1, zd, b), (zu, 0, zu, a),
            (z2, 0, z2, a), (z2, 1, z2, b),
        ]

    def _rows(self, first):
        return self.buf.at[pl.ds(pl.multiple_of(first, 32), 32)]

    def _copy(self, i, received):
        sent, half, got, to = self.t[i]
        if isinstance(to, tuple):
            base, dev = to
            dst = self._rows(base * OWN + got * 32)
            src = dst if received else self._rows(sent * OWN + half * 32)
        else:
            dev = to
            dst = self._rows((got if received else sent) * OWN + half * 32)
            src = dst
        return remote(src, dst, self.ss.at[i], self.rs.at[i], dev)

    def send(self, *idx):
        for i in idx:
            self._copy(i, False).start()

    def recv(self, *idx):
        for i in idx:
            self._copy(i, True).wait_recv()

    def s0(self):
        self.send(0, 1, 4, 5, 2, 3)

    def s1(self):
        self.recv(0)
        self.send(6, 7)
        self.recv(1)
        self.send(8, 9)

    def s2(self):
        self.recv(2)
        self.send(10)
        self.recv(3)
        self.send(11)

    def s3(self):
        self.recv(6)
        self.send(12)
        self.recv(8)
        self.send(13)

    def s4(self):
        self.recv(4, 5, 7, 9, 10, 11, 12, 13)

    def drain(self):
        for i in range(14):
            self._copy(i, False).wait_send()


class DpGather:
    def __init__(self, p, buf, ss, rs, rows):
        x, h, c, xu, xd, x2, o, g = p.x, p.h, p.c, p.xu, p.xd, p.x2, 1 - p.h, 1 - p.c
        up, dn = {"dp": dp_of(xu, h, c)}, {"dp": dp_of(xd, h, c)}
        pair, core = {"dp": dp_of(x, o, c)}, {"dp": dp_of(x, h, g)}
        self.buf, self.ss, self.rs = buf, ss, rs
        r, hf = rows, rows // 2
        self.t = [
            ((x, h, c), (x, h, g), 0, r, core),
            ((x, h, c), (x, o, c), 0, r, pair),
            ((x, h, c), (xd, h, c), 0, r, up),
            ((x, h, c), (xu, h, c), 0, r, dn),
            ((x, o, c), (xd, o, c), 0, r, up),
            ((x, o, c), (xu, o, c), 0, r, dn),
            ((xd, h, c), (x2, h, c), 0, hf, up),
            ((xu, h, c), (x2, h, c), hf, hf, dn),
            ((xd, o, c), (x2, o, c), 0, hf, up),
            ((xu, o, c), (x2, o, c), hf, hf, dn),
            ((x, o, c), (x, o, g), 0, r, core),
            ((xd, h, c), (xd, h, g), 0, r, core),
            ((xu, h, c), (xu, h, g), 0, r, core),
            ((xd, o, c), (xd, o, g), 0, r, core),
            ((xu, o, c), (xu, o, g), 0, r, core),
            ((x2, h, c), (x2, h, g), 0, r, core),
            ((x2, o, c), (x2, o, g), 0, r, core),
        ]

    def _copy(self, i, received, src=None):
        sent, got, first, n, to = self.t[i]
        sx, sh, sc = got if received else sent
        ref = self.buf.at[sc, sx * 2 + sh, pl.ds(first, n)]
        return remote(ref if src is None else src, ref, self.ss.at[i], self.rs.at[i], to)

    def send(self, *idx, src=None):
        for i in idx:
            self._copy(i, False, src).start()

    def recv(self, *idx):
        for i in idx:
            self._copy(i, True).wait_recv()

    def s0(self, src=None):
        self.send(1, 2, 3, 0, src=src)

    def fwd(self, *ks):
        for k in ks:
            if k < 6:
                self.recv(k)
                if k == 1:
                    self.send(4, 5, 10)
                else:
                    self.send(k + 4, k + 9)
            elif k == 6:
                self.recv(6, 7)
                self.send(15)
            else:
                self.recv(8, 9)
                self.send(16)

    def done(self, *ks):
        for k in ks:
            self.recv(k + 9 if k else 0)

    def drain(self):
        for i in range(17):
            self._copy(i, False).wait_send()


class RingReduce:
    def __init__(self, part, far, near, ysend, yrecv, ss, rs, ring, pair, up, dn, mate):
        self.part, self.far, self.near, self.ysend, self.yrecv = part, far, near, ysend, yrecv
        self.ss, self.rs = ss, rs
        self.r, self.ru, self.rd, self.r2 = ring
        self.l, self.m = pair, 1 - pair
        self.up, self.dn, self.mate = up, dn, mate

    def _copy(self, i, k):
        p = self.part(k)
        src, dst, to = [
            (lambda: p.at[self.r2 * 2], lambda: self.far.at[k, 0], self.up),
            (lambda: p.at[self.r2 * 2 + 1], lambda: self.far.at[k, 1], self.dn),
            (lambda: p.at[self.ru * 2 + 1], lambda: self.near.at[k, 1], self.up),
            (lambda: p.at[self.rd * 2], lambda: self.near.at[k, 2], self.dn),
            (lambda: p.at[self.ru * 2], lambda: self.near.at[k, 0], self.up),
            (lambda: p.at[self.rd * 2 + 1], lambda: self.near.at[k, 3], self.dn),
            (lambda: self.ysend.at[k], lambda: self.yrecv.at[k], self.mate),
        ][i]
        return remote(src(), dst(), self.ss.at[k, i], self.rs.at[k, i], to)

    def stage1(self, k):
        for i in range(4):
            self._copy(i, k).start()

    def stage2(self, k):
        p = self.part(k)
        for i, blk in ((0, self.ru * 2), (1, self.rd * 2 + 1)):
            self._copy(i, k).wait_recv()
            p[blk] = (p[blk].astype(F32) + self.far[k, i].astype(F32)).astype(BF)
            self._copy(4 + i, k).start()

    def stage3(self, k):
        for i in (2, 3, 4, 5):
            self._copy(i, k).wait_recv()
        p = self.part(k)

        def total(pair):
            return (
                p[self.r * 2 + pair].astype(F32)
                + self.near[k, pair].astype(F32)
                + self.near[k, 2 + pair].astype(F32)
            )

        self.ysend[k] = total(self.m).astype(BF)
        self._copy(6, k).start()
        return total(self.l)

    def stage4(self, k):
        self._copy(6, k).wait_recv()
        return self.yrecv[k].astype(F32)

    def drain(self, n):
        def body(k, _):
            for i in range(7):
                self._copy(i, k).wait_send()
            return 0

        lax.fori_loop(0, n, body, 0)


class ColumnReduce:
    def __init__(self, p, part, near, far, side, ss, rs, up, dn, mate_a, mate_b):
        self.z, self.zu, self.zd, self.z2 = p.z, p.zu, p.zd, p.z2
        self.part, self.near, self.far, self.side = part, near, far, side
        self.ss, self.rs = ss, rs
        self.up, self.dn, self.a, self.b = up, dn, mate_a, mate_b

    def _copy(self, i, k):
        lo, hi = pl.ds(0, 32), pl.ds(32, 32)
        src, dst, to = [
            (lambda: self.part.at[k, pl.ds(4, 2)], lambda: self.side.at[k, pl.ds(0, 2)], self.a),
            (lambda: self.part.at[k, pl.ds(6, 2)], lambda: self.side.at[k, pl.ds(2, 2)], self.b),
            (lambda: self.part.at[k, self.z2, lo], lambda: self.far.at[k, 0, lo], self.up),
            (lambda: self.part.at[k, self.z2, hi], lambda: self.far.at[k, 1, lo], self.dn),
            (lambda: self.part.at[k, self.zu, hi], lambda: self.near.at[k, 0, hi], self.up),
            (lambda: self.part.at[k, self.zd, lo], lambda: self.near.at[k, 1, lo], self.dn),
            (lambda: self.part.at[k, self.zu, lo], lambda: self.near.at[k, 0, lo], self.up),
            (lambda: self.part.at[k, self.zd, hi], lambda: self.near.at[k, 1, hi], self.dn),
        ][i]
        return remote(src(), dst(), self.ss.at[k, i], self.rs.at[k, i], to)

    def stage1(self, k):
        self._copy(0, k).start()
        self._copy(1, k).start()

    def stage2(self, k):
        for i in range(2):
            self._copy(i, k).wait_recv()
            rows = pl.ds(32 * i, 32)
            for zz in range(4):
                got = self.side[k, 2 * i + zz // 2, pl.ds(32 * (zz % 2), 32)]
                self.part[k, zz, rows] = (
                    self.part[k, zz, rows].astype(F32) + got.astype(F32)
                ).astype(BF)
        for i in range(2, 6):
            self._copy(i, k).start()

    def stage3(self, k):
        for i, blk in ((0, self.zu), (1, self.zd)):
            self._copy(2 + i, k).wait_recv()
            rows = pl.ds(32 * i, 32)
            self.part[k, blk, rows] = (
                self.part[k, blk, rows].astype(F32) + self.far[k, i, pl.ds(0, 32)].astype(F32)
            ).astype(BF)
            self._copy(6 + i, k).start()

    def stage4(self, k):
        for i in range(4, 8):
            self._copy(i, k).wait_recv()
        return (
            self.part[k, self.z].astype(F32)
            + self.near[k, 0].astype(F32)
            + self.near[k, 1].astype(F32)
        )

    def drain(self, n):
        def body(k, _):
            for i in range(8):
                self._copy(i, k).wait_send()
            return 0

        lax.fori_loop(0, n, body, 0)


def kernel(
    stream, final_gain, residual, ffn_gain, queries, keys, values, ctx, key_w, value_w,
    gate_hbm, up_hbm, down_hbm,
    out_ref, qg_ref, kwg_ref, vwg_ref, down_all,
    res_g, str_g, ffn_g, kvw, gate_v, up_v, down_v, part, far, near, ysend, yrecv,
    inear, coef_a, coef_b, ggrad, ugrad, acc, sgrad, kvg, kvg_t,
    crecv, wfar, wnear, wysend, wyrecv, wacc,
    res_ss, res_rs, str_ss, str_rs, ffn_ss, ffn_rs, kv_ss, kv_rs, dn_ss, dn_rs,
    er_ss, er_rs, ir_ss, ir_rs, wr_ss, wr_rs, cs_ss, cs_rs, loc, dsem,
):
    p = Place()
    MESH = pl.DeviceIdType.MESH
    z_up, z_dn = {"tensor": tn_of(p.zu, p.l)}, {"tensor": tn_of(p.zd, p.l)}
    mate = {"tensor": tn_of(p.z, 1 - p.l)}
    x_up, x_dn = {"dp": dp_of(p.xu, p.h, p.c)}, {"dp": dp_of(p.xd, p.h, p.c)}
    mate_b = {"dp": dp_of(p.x, 1 - p.h, p.c), "tensor": tn_of(p.z, 1 - p.l)}
    h_mate, core = {"dp": dp_of(p.x, 1 - p.h, p.c)}, {"dp": dp_of(p.x, p.h, 1 - p.c)}

    barrier = pltpu.get_barrier_semaphore()
    for dev in (z_up, z_dn, mate, mate_b, x_up, x_dn, h_mate, core):
        pl.semaphore_signal(barrier, inc=1, device_id=dev, device_id_type=MESH)

    own_chip = p.x * 2 + p.h
    gate_load = pltpu.make_async_copy(gate_hbm, gate_v, loc.at[0])
    up_load = pltpu.make_async_copy(up_hbm, up_v, loc.at[1])
    down_in = pltpu.make_async_copy(down_hbm, crecv.at[0], loc.at[2])
    down_in.start()
    down_own = pltpu.make_async_copy(crecv.at[0], down_all.at[p.c, own_chip], loc.at[3])
    gate_load.start()
    up_load.start()

    kvw[p.c, own_chip, 0:HD, :] = key_w[...]
    kvw[p.c, own_chip, HD : 2 * HD, :] = value_w[...]
    own = pl.multiple_of(p.tn * OWN, OWN)
    own_z = pl.multiple_of(p.z * OWN, OWN)

    def normed(src, gain, dst, at):
        def body(i, _):
            r = pl.multiple_of(i * 16, 16)
            v = src[pl.ds(r, 16), :].astype(F32)
            s = lax.rsqrt(jnp.mean(v * v, axis=-1, keepdims=True) + 1e-06)
            dst[pl.ds(pl.multiple_of(at + r, 16), 16), :] = (v * s * gain[...]).astype(BF)
            return 0

        lax.fori_loop(0, OWN // 16, body, 0)

    kv = DpGather(p, kvw, kv_ss, kv_rs, 2 * HD)
    down = DpGather(p, down_all, dn_ss, dn_rs, FFL // WR)
    res = ColumnGather(p, res_g, res_ss, res_rs, z_up, z_dn, mate, mate_b)
    stm = TensorGather(p, str_g, str_ss, str_rs)
    ffn = ColumnGather(p, ffn_g, ffn_ss, ffn_rs, z_up, z_dn, mate, mate_b)

    pl.semaphore_wait(barrier, 8)
    kv.s0()
    normed(residual, ffn_gain, res_g, own_z)
    res.s0()
    normed(stream, final_gain, str_g, own)

    s_t = dot(keys[...], queries[...], NT)
    e_t = jnp.exp(s_t - jnp.max(s_t, axis=0, keepdims=True))
    probs = e_t / jnp.sum(e_t, axis=0, keepdims=True)
    pg = dot(values[...], ctx[...], NT)
    delta = jnp.sum(probs * pg, axis=0, keepdims=True)
    sg = (probs * (pg - delta)).astype(BF)
    vgrad = dot(probs.astype(BF), ctx[...])
    kgrad = dot(sg, queries[...])
    kvg[:, 0:HD] = kgrad.astype(BF)
    kvg[:, HD : 2 * HD] = vgrad.astype(BF)
    kvg_t[0:HD, :] = kgrad.T.astype(BF)
    kvg_t[HD : 2 * HD, :] = vgrad.T.astype(BF)
    qg_ref[...] = dot(sg, keys[...], TN).astype(BF)

    down_in.wait()
    down_own.start()

    ring_z = (p.z, p.zu, p.zd, p.z2)
    ring_x = (p.x, p.xu, p.xd, p.x2)
    enc_rs = RingReduce(
        lambda k: part.at[k], far, near, ysend, yrecv, er_ss, er_rs, ring_z, p.l, z_up, z_dn, mate
    )
    in_rs = ColumnReduce(
        p, part, inear, far, near, ir_ss, ir_rs, z_up, z_dn, mate, mate_b
    )
    w_rs = RingReduce(
        lambda k: kvw.at[p.c, :, pl.ds(pl.multiple_of(k * WR, WR), WR), :],
        wfar, wnear, wysend, wyrecv, wr_ss, wr_rs, ring_x, p.h, x_up, x_dn, h_mate,
    )

    def chunk_of(k):
        if isinstance(k, int):
            return [
                p.x * 2 + p.h, p.x * 2 + 1 - p.h, p.xd * 2 + p.h, p.xu * 2 + p.h,
                p.xd * 2 + 1 - p.h, p.xu * 2 + 1 - p.h, p.x2 * 2 + p.h, p.x2 * 2 + 1 - p.h,
            ][k]
        raise TypeError

    def start_down():
        down_own.wait()
        down.s0()

    def enc_compute(k):
        chip = chunk_of(k)
        for cc in range(2):
            blk = dot(kvg[:, 0:HD], kvw[cc, chip, 0:HD, :], NT)
            blk = blk + dot(kvg[:, HD : 2 * HD], kvw[cc, chip, HD : 2 * HD, :], NT)
            part[k, :, :, cc * HD : (cc + 1) * HD] = blk.astype(BF).reshape(8, OWN, HD)

    lag = 4
    before = {
        1: lambda: kv.fwd(1),
        2: lambda: kv.fwd(2, 3),
        4: lambda: kv.fwd(4, 5),
        6: lambda: kv.fwd(6),
        7: lambda: kv.fwd(7),
    }
    after = {
        2: res.s1,
        4: start_down,
        5: res.s2,
        7: res.s3,
        9: lambda: down.fwd(1),
        11: lambda: down.fwd(2, 3),
    }
    for k in range(NCH + 2 + lag):
        if k in before:
            before[k]()
        if k < NCH:
            kv.done(k)
            enc_compute(k)
            enc_rs.stage1(k)
        if k in after:
            after[k]()
        if 0 <= k - lag < NCH:
            enc_rs.stage2(k - lag)
        if 0 <= k - lag - 1 < NCH:
            acc[k - lag - 1] = enc_rs.stage3(k - lag - 1)
        if 0 <= k - lag - 2 < NCH:
            acc[k - lag - 2] = acc[k - lag - 2] + enc_rs.stage4(k - lag - 2)

    def cols(k):
        start = chunk_of(k) * CW
        return pl.ds(pl.multiple_of(start, CW), CW)

    sq = jnp.zeros((OWN, 1), F32)
    ip = jnp.zeros((OWN, 1), F32)
    for k in range(NCH):
        v = stream[:, cols(k)].astype(F32)
        sq = sq + jnp.sum(v * v, axis=-1, keepdims=True)
        ip = ip + jnp.sum(acc[k] * final_gain[:, cols(k)] * v, axis=-1, keepdims=True)
    scale = lax.rsqrt(sq * (1.0 / D) + 1e-06)
    mix = scale * scale * scale * (ip * (1.0 / D))
    for k in range(NCH):
        v = stream[:, cols(k)].astype(F32)
        grad = scale * (acc[k] * final_gain[:, cols(k)]) - v * mix
        sgrad[:, cols(k)] = grad
        ffn_g[pl.ds(own_z, OWN), cols(k)] = grad.astype(BF)
    ffn.s0()

    gate_load.wait()
    up_load.wait()
    res.s4()

    def gate_tile(j):
        c0 = pl.ds(pl.multiple_of(j * HD, HD), HD)
        gate = dot(res_g[...], gate_v[:, c0])
        up = dot(res_g[...], up_v[:, c0])
        sig = 1.0 / (1.0 + jnp.exp(-gate))
        coef_a[:, c0] = (up * sig * (1.0 + gate * (1.0 - sig))).astype(BF)
        coef_b[:, c0] = (gate * sig).astype(BF)

    def gate_tiles(lo, hi):
        lax.fori_loop(lo, hi, lambda j, _: (gate_tile(j), 0)[1], 0)

    gate_tiles(0, 1)
    down.fwd(4, 5)
    ffn.s1()
    stm.s0()
    gate_tiles(1, 2)
    ffn.s2()
    gate_tiles(2, 3)
    down.fwd(6, 7)
    ffn.s3()
    stm.s1()
    gate_tiles(3, 4)
    down.done(*range(8))

    def w_tile(chip, _):
        for cc in range(2):
            c0 = pl.ds(pl.multiple_of((chip * 2 + cc) * HD, HD), HD)
            kvw[cc, chip] = dot(kvg_t[...], str_g[:, c0]).astype(BF)
        return 0

    def down_load(j):
        s = j % 2
        return pltpu.make_async_copy(
            down_all.at[:, :, pl.ds(j * 2, 2)], down_v.at[s], dsem.at[s]
        )

    down_load(0).start()

    def core_copy(k):
        rows = pl.ds(pl.multiple_of(k * WR, WR), WR)
        return remote(
            kvw.at[1 - p.c, :, rows, :], crecv.at[k], cs_ss.at[k], cs_rs.at[k], core
        )

    enc_rs.drain(NCH)
    kv.drain()
    stm.s2()
    ffn.s4()

    def hidden_tile(j, _):
        @pl.when(j < 3)
        def _():
            down_load(j + 1).start()

        down_load(j).wait()
        s = j % 2
        hid = jnp.zeros((TOK, HD), F32)
        for i in range(16):
            hid = hid + dot(ffn_g[:, i * HD : (i + 1) * HD], down_v[s, i % 2, i // 2].reshape(HD, HD), NT)
        c0 = pl.ds(pl.multiple_of(j * HD, HD), HD)
        ggrad[:, c0] = (hid * coef_a[:, c0].astype(F32)).astype(BF)
        ugrad[:, c0] = (hid * coef_b[:, c0].astype(F32)).astype(BF)
        return 0

    lax.fori_loop(0, 4, hidden_tile, 0)

    def in_step(k, _):
        @pl.when(k < NCH)
        def _():
            rows = pl.ds(pl.multiple_of(k * CW, CW), CW)
            blk = dot(ggrad[...], gate_v[rows, :], NT) + dot(ugrad[...], up_v[rows, :], NT)
            part[k] = blk.astype(BF).reshape(8, OWN, CW)
            in_rs.stage1(k)

        @pl.when(k == 1)
        def _():
            stm.s3()

        @pl.when(k == W0)
        def _():
            stm.s4()
            lax.fori_loop(0, 8, w_tile, 0)
            for i in range(WCH):
                core_copy(i).start()

        w = k - W0 - 1

        @pl.when((w >= 0) & (w < WCH))
        def _():
            core_copy(w).wait_recv()
            mine = w_rs.part(w)
            mine[...] = (mine[...].astype(F32) + crecv[w].astype(F32)).astype(BF)
            w_rs.stage1(w)

        @pl.when((k >= 1) & (k < NCH + 1))
        def _():
            in_rs.stage2(k - 1)

        @pl.when((w >= 1) & (w < WCH + 1))
        def _():
            w_rs.stage2(w - 1)

        @pl.when((k >= 2) & (k < NCH + 2))
        def _():
            in_rs.stage3(k - 2)

        @pl.when((w >= 2) & (w < WCH + 2))
        def _():
            wacc[w - 2] = w_rs.stage3(w - 2)

        @pl.when((k >= 3) & (k < NCH + 3))
        def _():
            acc[k - 3] = in_rs.stage4(k - 3)

        @pl.when((w >= 3) & (w < WCH + 3))
        def _():
            wacc[w - 3] = wacc[w - 3] + w_rs.stage4(w - 3)

        return 0

    lax.fori_loop(0, max(NCH + 3, W0 + WCH + 4), in_step, 0)

    for half in range(2):
        kwg_ref[:, half * WR : (half + 1) * WR] = wacc[half].T.astype(BF)
        vwg_ref[:, half * WR : (half + 1) * WR] = wacc[2 + half].T.astype(BF)

    sq = jnp.zeros((OWN, 1), F32)
    ip = jnp.zeros((OWN, 1), F32)
    for k in range(NCH):
        c0 = slice(k * CW, (k + 1) * CW)
        v = residual[:, c0].astype(F32)
        sq = sq + jnp.sum(v * v, axis=-1, keepdims=True)
        ip = ip + jnp.sum(acc[k] * ffn_gain[:, c0] * v, axis=-1, keepdims=True)
    scale = lax.rsqrt(sq * (1.0 / D) + 1e-06)
    mix = scale * scale * scale * (ip * (1.0 / D))
    for k in range(NCH):
        c0 = slice(k * CW, (k + 1) * CW)
        v = residual[:, c0].astype(F32)
        out_ref[:, c0] = (
            sgrad[:, c0] + scale * (acc[k] * ffn_gain[:, c0]) - v * mix
        ).astype(BF)

    for g in (res, stm, ffn, down):
        g.drain()
    in_rs.drain(NCH)
    w_rs.drain(WCH)
    for k in range(WCH):
        core_copy(k).wait_send()


def place_results(*refs):
    for src, dst in zip(refs[:4], refs[4:]):
        dst[...] = src[...]


def local(
    stream, final_gain, residual, ffn_gain, queries, saved_keys, saved_values, context_grad,
    key_weight, value_weight, gate_weight, up_weight, down_weight,
):
    vm = pl.BlockSpec(memory_space=pltpu.VMEM)
    hbm = pl.BlockSpec(memory_space=pl.ANY)
    dma = pltpu.SemaphoreType.DMA
    sds = jax.ShapeDtypeStruct
    v = pltpu.VMEM
    outs = pl.pallas_call(
        kernel,
        out_shape=(
            sds((OWN, D), BF), sds((Q, HD), BF), sds((HD, HD), BF), sds((HD, HD), BF),
            sds((2, 8, FFL // WR, WR, HD), BF),
        ),
        in_specs=[vm] * 10 + [hbm] * 3,
        out_specs=(vm, vm, vm, vm, hbm),
        scratch_shapes=[
            v((TOK, D), BF), v((TOK, D), BF), v((TOK, D), BF),
            v((2, 8, 2 * HD, HD), BF),
            v((D, FFL), BF), v((D, FFL), BF),
            v((2, 2, 8, 2, WR, HD), BF),
            v((NCH, 8, OWN, CW), BF),
            v((NCH, 2, OWN, CW), BF), v((NCH, 4, OWN, CW), BF),
            v((NCH, OWN, CW), BF), v((NCH, OWN, CW), BF),
            v((NCH, 2, OWN, CW), BF),
            v((TOK, FFL), BF), v((TOK, FFL), BF), v((TOK, FFL), BF), v((TOK, FFL), BF),
            v((NCH, OWN, CW), F32), v((OWN, D), F32),
            v((TOK, 2 * HD), BF), v((2 * HD, TOK), BF),
            v((WCH, 8, WR, HD), BF),
            v((WCH, 2, WR, HD), BF), v((WCH, 4, WR, HD), BF),
            v((WCH, WR, HD), BF), v((WCH, WR, HD), BF), v((WCH, WR, HD), F32),
            dma((14,)), dma((14,)), dma((9,)), dma((9,)), dma((14,)), dma((14,)),
            dma((17,)), dma((17,)), dma((17,)), dma((17,)),
            dma((NCH, 7)), dma((NCH, 7)), dma((NCH, 8)), dma((NCH, 8)),
            dma((WCH, 7)), dma((WCH, 7)), dma((WCH,)), dma((WCH,)),
            dma((4,)), dma((2,)),
        ],
        compiler_params=pltpu.CompilerParams(
            collective_id=0, has_side_effects=True, vmem_limit_bytes=64 * 1024 * 1024
        ),
        name="cross_ffn_backward",
    )(
        stream, final_gain.reshape(1, D), residual, ffn_gain.reshape(1, D), queries, saved_keys,
        saved_values, context_grad, key_weight, value_weight, gate_weight, up_weight,
        down_weight.reshape(FFL // WR, WR, HD),
    )
    return pl.pallas_call(
        place_results,
        out_shape=tuple(sds(o.shape, o.dtype) for o in outs[:4]),
        in_specs=[vm] * 4,
        out_specs=(vm,) * 4,
        name="place_results",
    )(*outs[:4])


def solution(mesh):
    return jax.shard_map(
        local,
        mesh=mesh,
        in_specs=(
            P(("dp", "tensor"), None), P(), P(("dp", "tensor"), None), P(),
            P("dp", "tensor"), P("dp", "tensor"), P("dp", "tensor"), P("dp", "tensor"),
            P("dp", "tensor"), P("dp", "tensor"), P(None, "tensor"), P(None, "tensor"),
            P("tensor", "dp"),
        ),
        out_specs=(
            P(("dp", "tensor"), None), P("dp", "tensor"), P("dp", "tensor"), P("dp", "tensor"),
        ),
        check_vma=False,
    )
```

```python
import jax
import jax.numpy as jnp
from jax import lax
from jax.experimental import pallas as pl
from jax.experimental.pallas import tpu as pltpu
from jax.sharding import PartitionSpec as P

BF = jnp.bfloat16
F32 = jnp.float32
D, TOK, OWN, FFL, HD, Q = 4096, 512, 64, 1024, 256, 256
NCH, CW = 8, 512
TH = TOK // 2
NQ = 2 * NCH
HALF, QTR = OWN // 2, OWN // 4
WCH, WR = 4, 128
ARRIVAL = (0, 2, 3, 6, 1, 4, 5, 7)
LE, LI, LW = 5, 6, 4
S2, S3 = 2, 6
W0 = 11

NN = (((1,), (0,)), ((), ()))
NT = (((1,), (1,)), ((), ()))
TN = (((0,), (0,)), ((), ()))


def dot(a, b, dims=NN):
    return lax.dot_general(a, b, dims, preferred_element_type=F32)


class Place:
    def __init__(self):
        dp, tn = lax.axis_index("dp"), lax.axis_index("tensor")
        self.dp, self.tn = dp, tn
        self.x, self.h, self.c = dp // 4, (dp // 2) % 2, dp % 2
        self.z, self.l = tn // 2, tn % 2
        self.xu, self.xd, self.x2 = (self.x + 1) % 4, (self.x + 3) % 4, (self.x + 2) % 4
        self.zu, self.zd, self.z2 = (self.z + 1) % 4, (self.z + 3) % 4, (self.z + 2) % 4


def dp_of(x, h, c):
    return (x * 2 + h) * 2 + c


def tn_of(z, l):
    return z * 2 + l


def remote(src, dst, ss, rs, dev):
    return pltpu.make_async_remote_copy(
        src_ref=src, dst_ref=dst, send_sem=ss, recv_sem=rs, device_id=dev,
        device_id_type=pl.DeviceIdType.MESH,
    )


class TensorGather:
    def __init__(self, p, buf, ss, rs):
        z, l, zu, zd, z2, m = p.z, p.l, p.zu, p.zd, p.z2, 1 - p.l
        up, dn, pair = {"tensor": tn_of(zu, l)}, {"tensor": tn_of(zd, l)}, {"tensor": tn_of(z, m)}
        self.buf, self.ss, self.rs = buf, ss, rs
        self.t = [
            ((z, l), (z, m), 0, 64, pair),
            ((z, l), (zd, l), 0, 64, up),
            ((z, l), (zu, l), 0, 64, dn),
            ((z, m), (zd, m), 0, 64, up),
            ((z, m), (zu, m), 0, 64, dn),
            ((zd, l), (z2, l), 0, 32, up),
            ((zu, l), (z2, l), 32, 32, dn),
            ((zd, m), (z2, m), 0, 32, up),
            ((zu, m), (z2, m), 32, 32, dn),
        ]

    def _copy(self, i, received):
        sent, got, first, n, to = self.t[i]
        at = tn_of(*(got if received else sent)) * OWN + first
        ref = self.buf.at[pl.ds(pl.multiple_of(at, 16), n)]
        return remote(ref, ref, self.ss, self.rs.at[i], to)

    def send(self, *idx):
        for i in idx:
            self._copy(i, False).start()

    def recv(self, *idx):
        for i in idx:
            self._copy(i, True).wait_recv()

    def s0(self):
        self.send(1, 2, 0)

    def s1(self):
        self.recv(0)
        self.send(3, 4)

    def s2(self):
        self.recv(1)
        self.send(5)
        self.recv(2)
        self.send(6)

    def s3(self):
        self.recv(3)
        self.send(7)
        self.recv(4)
        self.send(8)

    def s4(self):
        self.recv(5, 6, 7, 8)

    def drain(self):
        sent = self.buf.at[pl.ds(0, 448)]
        remote(sent, sent, self.ss, self.rs.at[0], self.t[0][4]).wait_send()


class ColumnGather:
    def __init__(self, p, buf, base, ss, rs, up, dn, mate_a, mate_b):
        z, zu, zd, z2 = p.z, p.zu, p.zd, p.z2
        self.buf, self.base, self.ss, self.rs = buf, base, ss, rs
        a, b = (4, mate_a), (6, mate_b)
        self.t = [
            (z, 0, zd, up), (z, 1, zu, dn), (z, 1, zd, up), (z, 0, zu, dn),
            (z, 0, z, a), (z, 1, z, b),
            (zd, 0, z2, up), (zd, 0, zd, a),
            (zu, 1, z2, dn), (zu, 1, zu, b),
            (zd, 1, zd, b), (zu, 0, zu, a),
            (z2, 0, z2, a), (z2, 1, z2, b),
        ]

    def _rows(self, first):
        return self.buf.at[pl.ds(pl.multiple_of(self.base + first, 16), QTR)]

    def _copy(self, i, received):
        sent, half, got, to = self.t[i]
        if isinstance(to, tuple):
            base, dev = to
            dst = self._rows(base * HALF + got * QTR)
            src = dst if received else self._rows(sent * HALF + half * QTR)
        else:
            dev = to
            dst = self._rows((got if received else sent) * HALF + half * QTR)
            src = dst
        return remote(src, dst, self.ss, self.rs.at[i], dev)

    def send(self, *idx):
        for i in idx:
            self._copy(i, False).start()

    def recv(self, *idx):
        for i in idx:
            self._copy(i, True).wait_recv()

    def s0(self):
        self.send(0, 1, 2, 3, 4, 5)

    def s1(self):
        self.recv(0)
        self.send(6, 7)
        self.recv(1)
        self.send(8, 9)

    def s2(self):
        self.recv(2)
        self.send(10)
        self.recv(3)
        self.send(11)

    def s3(self):
        self.recv(6)
        self.send(12)
        self.recv(8)
        self.send(13)

    def s4(self):
        self.recv(4, 5, 7, 9, 10, 11, 12, 13)

    def drain(self):
        sent = self.buf.at[pl.ds(0, 14 * QTR)]
        remote(sent, sent, self.ss, self.rs.at[0], self.t[0][3]).wait_send()


class DpGather:
    def __init__(self, p, buf, ss, rs, rows):
        x, h, c, xu, xd, x2, o, g = p.x, p.h, p.c, p.xu, p.xd, p.x2, 1 - p.h, 1 - p.c
        up, dn = {"dp": dp_of(xu, h, c)}, {"dp": dp_of(xd, h, c)}
        pair, core = {"dp": dp_of(x, o, c)}, {"dp": dp_of(x, h, g)}
        self.buf, self.ss, self.rs = buf, ss, rs
        r, hf = rows, rows // 2
        self.t = [
            ((x, h, c), (x, h, g), 0, r, core),
            ((x, h, c), (x, o, c), 0, r, pair),
            ((x, h, c), (xd, h, c), 0, r, up),
            ((x, h, c), (xu, h, c), 0, r, dn),
            ((x, o, c), (xd, o, c), 0, r, up),
            ((x, o, c), (xu, o, c), 0, r, dn),
            ((xd, h, c), (x2, h, c), 0, hf, up),
            ((xu, h, c), (x2, h, c), hf, hf, dn),
            ((xd, o, c), (x2, o, c), 0, hf, up),
            ((xu, o, c), (x2, o, c), hf, hf, dn),
            ((x, o, c), (x, o, g), 0, r, core),
            ((xd, h, c), (xd, h, g), 0, r, core),
            ((xu, h, c), (xu, h, g), 0, r, core),
            ((xd, o, c), (xd, o, g), 0, r, core),
            ((xu, o, c), (xu, o, g), 0, r, core),
            ((x2, h, c), (x2, h, g), 0, r, core),
            ((x2, o, c), (x2, o, g), 0, r, core),
        ]

    def _copy(self, i, received):
        sent, got, first, n, to = self.t[i]
        sx, sh, sc = got if received else sent
        ref = self.buf.at[sc, sx * 2 + sh, pl.ds(first, n)]
        return remote(ref, ref, self.ss.at[i // 10], self.rs.at[i], to)

    def send(self, *idx):
        for i in idx:
            self._copy(i, False).start()

    def recv(self, *idx):
        for i in idx:
            self._copy(i, True).wait_recv()

    def s0(self):
        self.send(1, 2, 3, 0)

    def fwd(self, *ks):
        for k in ks:
            if k < 6:
                self.recv(k)
                if k == 1:
                    self.send(4, 5, 10)
                else:
                    self.send(k + 4, k + 9)
            elif k == 6:
                self.recv(6, 7)
                self.send(15)
            else:
                self.recv(8, 9)
                self.send(16)

    def done(self, *ks):
        for k in ks:
            self.recv(k + 9 if k else 0)

    def drain(self):
        for i, n in enumerate((8, 7)):
            sent = self.buf.at[0, pl.ds(0, n)]
            remote(sent, sent, self.ss.at[i], self.rs.at[0], self.t[0][4]).wait_send()


class RingReduce:
    def __init__(self, part, far, near, ysend, yrecv, ss, rs, ring, pair, up, dn, mate):
        self.part, self.far, self.near, self.ysend, self.yrecv = part, far, near, ysend, yrecv
        self.ss, self.rs = ss, rs
        self.r, self.ru, self.rd, self.r2 = ring
        self.l, self.m = pair, 1 - pair
        self.up, self.dn, self.mate = up, dn, mate

    def _copy(self, i, k):
        p = self.part(k)
        src, dst, to = [
            (lambda: p.at[self.r2 * 2], lambda: self.far.at[k, 0], self.up),
            (lambda: p.at[self.r2 * 2 + 1], lambda: self.far.at[k, 1], self.dn),
            (lambda: p.at[self.ru * 2 + 1], lambda: self.near.at[k, 1], self.up),
            (lambda: p.at[self.rd * 2], lambda: self.near.at[k, 2], self.dn),
            (lambda: p.at[self.ru * 2], lambda: self.near.at[k, 0], self.up),
            (lambda: p.at[self.rd * 2 + 1], lambda: self.near.at[k, 3], self.dn),
            (lambda: self.ysend.at[k], lambda: self.yrecv.at[k], self.mate),
        ][i]
        return remote(src(), dst(), self.ss.at[i], self.rs.at[k, (0, 1, 2, 2, 2, 2, 3)[i]], to)

    def stage1(self, k):
        for i in range(4):
            self._copy(i, k).start()

    def stage2(self, k):
        p = self.part(k)
        for i, blk in ((0, self.ru * 2), (1, self.rd * 2 + 1)):
            self._copy(i, k).wait_recv()
            p[blk] = (p[blk].astype(F32) + self.far[k, i].astype(F32)).astype(BF)
            self._copy(4 + i, k).start()

    def stage3(self, k):
        near = self.near.at[k]
        remote(near, near, self.ss.at[2], self.rs.at[k, 2], self.up).wait_recv()
        p = self.part(k)

        def total(pair):
            return (
                p[self.r * 2 + pair].astype(F32)
                + self.near[k, pair].astype(F32)
                + self.near[k, 2 + pair].astype(F32)
            )

        self.ysend[k] = total(self.m).astype(BF)
        self._copy(6, k).start()
        return total(self.l)

    def stage4(self, k):
        self._copy(6, k).wait_recv()
        return self.yrecv[k].astype(F32)

    def drain(self):
        for i in range(7):
            remote(self.ysend, self.ysend, self.ss.at[i], self.rs.at[0, 3], self.up).wait_send()


class ColumnReduce:
    def __init__(self, p, part, near, far, side, ss, rs, up, dn, mate_a, mate_b):
        self.z, self.zu, self.zd, self.z2 = p.z, p.zu, p.zd, p.z2
        self.part, self.near, self.far, self.side = part, near, far, side
        self.ss, self.rs = ss, rs
        self.up, self.dn, self.a, self.b = up, dn, mate_a, mate_b

    def _copy(self, i, k):
        lo, hi = pl.ds(0, QTR), pl.ds(QTR, QTR)
        src, dst, to = [
            (lambda: self.part.at[k, pl.ds(4, 2)], lambda: self.side.at[k, pl.ds(0, 2)], self.a),
            (lambda: self.part.at[k, pl.ds(6, 2)], lambda: self.side.at[k, pl.ds(2, 2)], self.b),
            (lambda: self.part.at[k, self.z2, lo], lambda: self.far.at[k, 0, lo], self.up),
            (lambda: self.part.at[k, self.z2, hi], lambda: self.far.at[k, 1, lo], self.dn),
            (lambda: self.part.at[k, self.zu, hi], lambda: self.near.at[k, 0, hi], self.up),
            (lambda: self.part.at[k, self.zd, lo], lambda: self.near.at[k, 1, lo], self.dn),
            (lambda: self.part.at[k, self.zu, lo], lambda: self.near.at[k, 0, lo], self.up),
            (lambda: self.part.at[k, self.zd, hi], lambda: self.near.at[k, 1, hi], self.dn),
        ][i]
        return remote(src(), dst(), self.ss.at[i], self.rs.at[k, (0, 0, 1, 2, 3, 3, 3, 3)[i]], to)

    def stage1(self, k):
        self._copy(0, k).start()
        self._copy(1, k).start()

    def stage2(self, k):
        side = self.side.at[k]
        remote(side, side, self.ss.at[0], self.rs.at[k, 0], self.a).wait_recv()
        for i in range(2):
            rows = pl.ds(QTR * i, QTR)
            for zz in range(4):
                got = self.side[k, 2 * i + zz // 2, pl.ds(QTR * (zz % 2), QTR)]
                self.part[k, zz, rows] = (
                    self.part[k, zz, rows].astype(F32) + got.astype(F32)
                ).astype(BF)
        for i in range(2, 6):
            self._copy(i, k).start()

    def stage3(self, k):
        for i, blk in ((0, self.zu), (1, self.zd)):
            self._copy(2 + i, k).wait_recv()
            rows = pl.ds(QTR * i, QTR)
            self.part[k, blk, rows] = (
                self.part[k, blk, rows].astype(F32) + self.far[k, i, pl.ds(0, QTR)].astype(F32)
            ).astype(BF)
            self._copy(6 + i, k).start()

    def stage4(self, k):
        near = self.near.at[k]
        remote(near, near, self.ss.at[4], self.rs.at[k, 3], self.up).wait_recv()
        return (
            self.part[k, self.z].astype(F32)
            + self.near[k, 0].astype(F32)
            + self.near[k, 1].astype(F32)
        )

    def drain(self):
        for i in range(8):
            sent = self.side.at[:, pl.ds(0, 2)] if i < 2 else self.far.at[:, 0, pl.ds(0, QTR)]
            remote(sent, sent, self.ss.at[i], self.rs.at[0, 3], self.up).wait_send()


def kernel(
    stream, final_gain, residual, ffn_gain, queries, keys, values, ctx, key_w, value_w,
    gate_hbm, up_hbm, down_hbm,
    out_ref, qg_ref, kwg_ref, vwg_ref, down_all,
    res_g, str_g, ffn_g, kvw, gate_v, up_v, down_v, part, far, near, ysend, yrecv,
    inear, coef_a, coef_b, ggrad, ugrad, acc, sgrad, kvg, kvg_t,
    crecv, wfar, wnear, wysend, wyrecv, wacc,
    res_ss, res_rs, str_ss, str_rs, ffn_ss, ffn_rs, kv_ss, kv_rs, dn_ss, dn_rs,
    er_ss, er_rs, ir_ss, ir_rs, wr_ss, wr_rs, cs_ss, cs_rs, loc, dsem,
):
    p = Place()
    MESH = pl.DeviceIdType.MESH
    z_up, z_dn = {"tensor": tn_of(p.zu, p.l)}, {"tensor": tn_of(p.zd, p.l)}
    mate = {"tensor": tn_of(p.z, 1 - p.l)}
    x_up, x_dn = {"dp": dp_of(p.xu, p.h, p.c)}, {"dp": dp_of(p.xd, p.h, p.c)}
    mate_b = {"dp": dp_of(p.x, 1 - p.h, p.c), "tensor": tn_of(p.z, 1 - p.l)}
    h_mate, core = {"dp": dp_of(p.x, 1 - p.h, p.c)}, {"dp": dp_of(p.x, p.h, 1 - p.c)}

    barrier = pltpu.get_barrier_semaphore()
    for dev in (z_up, z_dn, mate, mate_b, x_up, x_dn, h_mate, core):
        pl.semaphore_signal(barrier, inc=1, device_id=dev, device_id_type=MESH)

    own_chip = p.x * 2 + p.h
    gate_load = pltpu.make_async_copy(gate_hbm, gate_v, loc.at[0])
    up_load = pltpu.make_async_copy(up_hbm, up_v, loc.at[1])
    down_in = pltpu.make_async_copy(down_hbm, crecv.at[0], loc.at[2])
    down_in.start()
    down_own = pltpu.make_async_copy(crecv.at[0], down_all.at[p.c, own_chip], loc.at[3])
    gate_load.start()
    up_load.start()

    kvw[p.c, own_chip, 0:HD, :] = key_w[...]
    kvw[p.c, own_chip, HD : 2 * HD, :] = value_w[...]
    own = pl.multiple_of(p.tn * OWN, OWN)

    def normed(src, gain, dst, at):
        def body(i, _):
            r = pl.multiple_of(i * 16, 16)
            v = src[pl.ds(r, 16), :].astype(F32)
            s = lax.rsqrt(jnp.mean(v * v, axis=-1, keepdims=True) + 1e-06)
            dst[pl.ds(pl.multiple_of(at(i), 16), 16), :] = (v * s * gain[...]).astype(BF)
            return 0

        lax.fori_loop(0, OWN // 16, body, 0)

    kv = DpGather(p, kvw, kv_ss, kv_rs, 2 * HD)
    down = DpGather(p, down_all, dn_ss, dn_rs, FFL // WR)
    def column_gather(buf, ss, rs):
        return [
            ColumnGather(p, buf, b * TH, ss.at[b], rs.at[b], z_up, z_dn, mate, mate_b)
            for b in range(2)
        ]

    res = column_gather(res_g, res_ss, res_rs)
    stm = TensorGather(p, str_g, str_ss, str_rs)
    ffn = column_gather(ffn_g, ffn_ss, ffn_rs)

    pl.semaphore_wait(barrier, 8)
    kv.s0()
    normed(residual, ffn_gain, res_g, lambda i: (i // 2) * TH + p.z * HALF + (i % 2) * 16)
    res[0].s0()
    res[1].s0()
    normed(stream, final_gain, str_g, lambda i: own + i * 16)

    s_t = dot(keys[...], queries[...], NT)
    e_t = jnp.exp(s_t - jnp.max(s_t, axis=0, keepdims=True))
    probs = e_t / jnp.sum(e_t, axis=0, keepdims=True)
    pg = dot(values[...], ctx[...], NT)
    delta = jnp.sum(probs * pg, axis=0, keepdims=True)
    sg = (probs * (pg - delta)).astype(BF)
    vgrad = dot(probs.astype(BF), ctx[...])
    kgrad = dot(sg, queries[...])
    kvg[:, 0:HD] = kgrad.astype(BF)
    kvg[:, HD : 2 * HD] = vgrad.astype(BF)
    kvg_t[0:HD, :] = kgrad.T.astype(BF)
    kvg_t[HD : 2 * HD, :] = vgrad.T.astype(BF)
    qg_ref[...] = dot(sg, keys[...], TN).astype(BF)

    down_in.wait()
    down_own.start()

    ring_z = (p.z, p.zu, p.zd, p.z2)
    ring_x = (p.x, p.xu, p.xd, p.x2)
    enc_rs = RingReduce(
        lambda k: part.at[k], far, near, ysend, yrecv, er_ss, er_rs, ring_z, p.l, z_up, z_dn, mate
    )
    in_rs = ColumnReduce(
        p, part, inear, far, near, ir_ss, ir_rs, z_up, z_dn, mate, mate_b
    )
    w_rs = RingReduce(
        lambda k: kvw.at[p.c, :, pl.ds(pl.multiple_of(k * WR, WR), WR), :],
        wfar, wnear, wysend, wyrecv, wr_ss, wr_rs, ring_x, p.h, x_up, x_dn, h_mate,
    )

    def chunk_of(k):
        return [
            p.x * 2 + p.h, p.x * 2 + 1 - p.h, p.xd * 2 + p.h, p.xu * 2 + p.h,
            p.xd * 2 + 1 - p.h, p.xu * 2 + 1 - p.h, p.x2 * 2 + p.h, p.x2 * 2 + 1 - p.h,
        ][ARRIVAL[k]]

    def start_down():
        down_own.wait()
        down.s0()

    def enc_compute(k):
        chip = chunk_of(k)
        for cc in range(2):
            blk = dot(kvg[:, 0:HD], kvw[cc, chip, 0:HD, :], NT)
            blk = blk + dot(kvg[:, HD : 2 * HD], kvw[cc, chip, HD : 2 * HD, :], NT)
            blk = blk.astype(BF).reshape(8, 2, HALF, HD)
            for b in range(2):
                part[b * NCH + k, :, :, cc * HD : (cc + 1) * HD] = blk[:, b]

    def cols(k):
        return pl.ds(pl.multiple_of(chunk_of(k) * CW, CW), CW)

    def stream_back(b):
        rows = slice(b * HALF, (b + 1) * HALF)
        sq = jnp.zeros((HALF, 1), F32)
        ip = jnp.zeros((HALF, 1), F32)
        for k in range(NCH):
            v = stream[rows, cols(k)].astype(F32)
            sq = sq + jnp.sum(v * v, axis=-1, keepdims=True)
            ip = ip + jnp.sum(
                acc[b * NCH + k] * final_gain[:, cols(k)] * v, axis=-1, keepdims=True
            )
        scale = lax.rsqrt(sq * (1.0 / D) + 1e-06)
        mix = scale * scale * scale * (ip * (1.0 / D))
        at = pl.ds(pl.multiple_of(b * TH + p.z * HALF, HALF), HALF)
        for k in range(NCH):
            v = stream[rows, cols(k)].astype(F32)
            grad = scale * (acc[b * NCH + k] * final_gain[:, cols(k)]) - v * mix
            sgrad[rows, cols(k)] = grad
            ffn_g[at, cols(k)] = grad.astype(BF)
        ffn[b].s0()

    lag = LE
    F0 = NCH - 1 + 3 * lag
    before = {
        1: lambda: kv.fwd(2, 3),
        3: lambda: kv.fwd(6),
        4: lambda: kv.fwd(1),
        5: lambda: kv.fwd(4, 5),
        7: lambda: kv.fwd(7),
    }
    after = [
        (2, res[0].s1), (3, res[1].s1), (5, start_down), (6, res[0].s2), (7, res[1].s2),
        (8, res[0].s3), (9, res[1].s3), (11, lambda: down.fwd(2, 3)), (12, lambda: down.fwd(1)),
        (F0 + 3, ffn[0].s1), (F0 + 4, lambda: down.fwd(4, 5)), (F0 + 5, ffn[0].s2),
        (F0 + 6, ffn[0].s3), (F0 + 7, lambda: down.fwd(6, 7)),
    ]

    def flush(k):
        while after and after[0][0] <= k:
            after.pop(0)[1]()

    for k in range(NQ + 3 * lag):
        if k in before:
            before[k]()
        if k < NCH:
            kv.done(ARRIVAL[k])
            enc_compute(k)
        if k < NQ:
            enc_rs.stage1(k)
        flush(k)
        if 0 <= k - lag < NQ:
            enc_rs.stage2(k - lag)
        if 0 <= k - 2 * lag < NQ:
            acc[k - 2 * lag] = enc_rs.stage3(k - 2 * lag)
        if 0 <= k - 3 * lag < NQ:
            acc[k - 3 * lag] = acc[k - 3 * lag] + enc_rs.stage4(k - 3 * lag)
        if k - 3 * lag == NCH - 1:
            stream_back(0)
    stream_back(1)
    stm.s0()

    gate_load.wait()
    up_load.wait()
    res[0].s4()
    res[1].s4()

    def gate_tile(j):
        c0 = pl.ds(pl.multiple_of(j * HD, HD), HD)
        gate = dot(res_g[...], gate_v[:, c0])
        up = dot(res_g[...], up_v[:, c0])
        sig = 1.0 / (1.0 + jnp.exp(-gate))
        coef_a[:, c0] = (up * sig * (1.0 + gate * (1.0 - sig))).astype(BF)
        coef_b[:, c0] = (gate * sig).astype(BF)

    def gate_tiles(lo, hi):
        lax.fori_loop(lo, hi, lambda j, _: (gate_tile(j), 0)[1], 0)

    gate_tiles(0, 1)
    flush(99)
    ffn[1].s1()
    gate_tiles(1, 2)
    ffn[1].s2()
    stm.s1()
    gate_tiles(2, 3)
    ffn[1].s3()
    gate_tiles(3, 4)
    down.done(*range(8))

    def w_tile(chip, _):
        for cc in range(2):
            c0 = pl.ds(pl.multiple_of((chip * 2 + cc) * HD, HD), HD)
            kvw[cc, chip] = dot(kvg_t[...], str_g[:, c0]).astype(BF)
        return 0

    def down_load(j):
        s = j % 2
        return pltpu.make_async_copy(
            down_all.at[:, :, pl.ds(j * 2, 2)], down_v.at[s], dsem.at[s]
        )

    down_load(0).start()

    def core_copy(k):
        rows = pl.ds(pl.multiple_of(k * WR, WR), WR)
        return remote(
            kvw.at[1 - p.c, :, rows, :], crecv.at[k], cs_ss, cs_rs.at[k], core
        )

    enc_rs.drain()
    kv.drain()
    ffn[0].s4()

    def hidden(b):
        rows = slice(b * TH, (b + 1) * TH)

        def tile(j, _):
            @pl.when(j < 3)
            def _():
                down_load(j + 1).start()

            down_load(j).wait()
            s = j % 2
            hid = jnp.zeros((TH, HD), F32)
            for i in range(16):
                hid = hid + dot(
                    ffn_g[rows, i * HD : (i + 1) * HD],
                    down_v[s, i % 2, i // 2].reshape(HD, HD), NT,
                )
            c0 = pl.ds(pl.multiple_of(j * HD, HD), HD)
            ggrad[rows, c0] = (hid * coef_a[rows, c0].astype(F32)).astype(BF)
            ugrad[rows, c0] = (hid * coef_b[rows, c0].astype(F32)).astype(BF)
            return 0

        lax.fori_loop(0, 4, tile, 0)

    hidden(0)
    down_load(0).start()

    def in_step(k, _):
        @pl.when(k == NCH)
        def _():
            ffn[1].s4()
            hidden(1)

        @pl.when(k < NQ)
        def _():
            rows = pl.ds(pl.multiple_of((k % NCH) * CW, CW), CW)
            toks = pl.ds(pl.multiple_of((k // NCH) * TH, TH), TH)
            blk = dot(ggrad[toks, :], gate_v[rows, :], NT) + dot(ugrad[toks, :], up_v[rows, :], NT)
            part[k] = blk.astype(BF).reshape(8, HALF, CW)
            in_rs.stage1(k)

        @pl.when(k == S2)
        def _():
            stm.s2()

        @pl.when(k == S3)
        def _():
            stm.s3()

        @pl.when(k == W0)
        def _():
            stm.s4()
            lax.fori_loop(0, 8, w_tile, 0)
            for i in range(WCH):
                core_copy(i).start()

        w = k - W0 - 1

        @pl.when((w >= 0) & (w < WCH))
        def _():
            core_copy(w).wait_recv()
            mine = w_rs.part(w)
            mine[...] = (mine[...].astype(F32) + crecv[w].astype(F32)).astype(BF)
            w_rs.stage1(w)

        @pl.when((k >= 1 * LI) & (k < NQ + 1 * LI))
        def _():
            in_rs.stage2(k - LI)

        @pl.when((w >= 1 * LW) & (w < WCH + 1 * LW))
        def _():
            w_rs.stage2(w - LW)

        @pl.when((k >= 2 * LI) & (k < NQ + 2 * LI))
        def _():
            in_rs.stage3(k - 2 * LI)

        @pl.when((w >= 2 * LW) & (w < WCH + 2 * LW))
        def _():
            wacc[w - 2 * LW] = w_rs.stage3(w - 2 * LW)

        @pl.when((k >= 3 * LI) & (k < NQ + 3 * LI))
        def _():
            acc[k - 3 * LI] = in_rs.stage4(k - 3 * LI)

        @pl.when((w >= 3 * LW) & (w < WCH + 3 * LW))
        def _():
            wacc[w - 3 * LW] = wacc[w - 3 * LW] + w_rs.stage4(w - 3 * LW)

        return 0

    lax.fori_loop(0, max(NQ + 3 * LI, W0 + 1 + WCH + 3 * LW), in_step, 0)

    for half in range(2):
        kwg_ref[:, half * WR : (half + 1) * WR] = wacc[half].T.astype(BF)
        vwg_ref[:, half * WR : (half + 1) * WR] = wacc[2 + half].T.astype(BF)

    for b in range(2):
        rows = slice(b * HALF, (b + 1) * HALF)
        sq = jnp.zeros((HALF, 1), F32)
        ip = jnp.zeros((HALF, 1), F32)
        for k in range(NCH):
            c0 = slice(k * CW, (k + 1) * CW)
            v = residual[rows, c0].astype(F32)
            sq = sq + jnp.sum(v * v, axis=-1, keepdims=True)
            ip = ip + jnp.sum(acc[b * NCH + k] * ffn_gain[:, c0] * v, axis=-1, keepdims=True)
        scale = lax.rsqrt(sq * (1.0 / D) + 1e-06)
        mix = scale * scale * scale * (ip * (1.0 / D))
        for k in range(NCH):
            c0 = slice(k * CW, (k + 1) * CW)
            v = residual[rows, c0].astype(F32)
            out_ref[rows, c0] = (
                sgrad[rows, c0] + scale * (acc[b * NCH + k] * ffn_gain[:, c0]) - v * mix
            ).astype(BF)

    for g in (*res, stm, *ffn, down):
        g.drain()
    in_rs.drain()
    w_rs.drain()
    remote(crecv, crecv, cs_ss, cs_rs.at[0], core).wait_send()


def place_results(*refs):
    for src, dst in zip(refs[:4], refs[4:]):
        dst[...] = src[...]


def local(
    stream, final_gain, residual, ffn_gain, queries, saved_keys, saved_values, context_grad,
    key_weight, value_weight, gate_weight, up_weight, down_weight,
):
    vm = pl.BlockSpec(memory_space=pltpu.VMEM)
    hbm = pl.BlockSpec(memory_space=pl.ANY)
    dma = pltpu.SemaphoreType.DMA
    sds = jax.ShapeDtypeStruct
    v = pltpu.VMEM
    outs = pl.pallas_call(
        kernel,
        out_shape=(
            sds((OWN, D), BF), sds((Q, HD), BF), sds((HD, HD), BF), sds((HD, HD), BF),
            sds((2, 8, FFL // WR, WR, HD), BF),
        ),
        in_specs=[vm] * 10 + [hbm] * 3,
        out_specs=(vm, vm, vm, vm, hbm),
        scratch_shapes=[
            v((TOK, D), BF), v((TOK, D), BF), v((TOK, D), BF),
            v((2, 8, 2 * HD, HD), BF),
            v((D, FFL), BF), v((D, FFL), BF),
            v((2, 2, 8, 2, WR, HD), BF),
            v((NQ, 8, HALF, CW), BF),
            v((NQ, 2, HALF, CW), BF), v((NQ, 4, HALF, CW), BF),
            v((NQ, HALF, CW), BF), v((NQ, HALF, CW), BF),
            v((NQ, 2, HALF, CW), BF),
            v((TOK, FFL), BF), v((TOK, FFL), BF), v((TOK, FFL), BF), v((TOK, FFL), BF),
            v((NQ, HALF, CW), F32), v((OWN, D), F32),
            v((TOK, 2 * HD), BF), v((2 * HD, TOK), BF),
            v((WCH, 8, WR, HD), BF),
            v((WCH, 2, WR, HD), BF), v((WCH, 4, WR, HD), BF),
            v((WCH, WR, HD), BF), v((WCH, WR, HD), BF), v((WCH, WR, HD), F32),
            dma((2,)), dma((2, 14)), dma, dma((9,)), dma((2,)), dma((2, 14)),
            dma((2,)), dma((17,)), dma((2,)), dma((17,)),
            dma((7,)), dma((NQ, 4)), dma((8,)), dma((NQ, 4)),
            dma((7,)), dma((WCH, 4)), dma, dma((WCH,)),
            dma((4,)), dma((2,)),
        ],
        compiler_params=pltpu.CompilerParams(
            collective_id=0, has_side_effects=True, vmem_limit_bytes=64 * 1024 * 1024
        ),
        name="cross_ffn_backward",
    )(
        stream, final_gain.reshape(1, D), residual, ffn_gain.reshape(1, D), queries, saved_keys,
        saved_values, context_grad, key_weight, value_weight, gate_weight, up_weight,
        down_weight.reshape(FFL // WR, WR, HD),
    )
    return pl.pallas_call(
        place_results,
        out_shape=tuple(sds(o.shape, o.dtype) for o in outs[:4]),
        in_specs=[vm] * 4,
        out_specs=(vm,) * 4,
        name="place_results",
    )(*outs[:4])


def solution(mesh):
    return jax.shard_map(
        local,
        mesh=mesh,
        in_specs=(
            P(("dp", "tensor"), None), P(), P(("dp", "tensor"), None), P(),
            P("dp", "tensor"), P("dp", "tensor"), P("dp", "tensor"), P("dp", "tensor"),
            P("dp", "tensor"), P("dp", "tensor"), P(None, "tensor"), P(None, "tensor"),
            P("tensor", "dp"),
        ),
        out_specs=(
            P(("dp", "tensor"), None), P("dp", "tensor"), P("dp", "tensor"), P("dp", "tensor"),
        ),
        check_vma=False,
    )
```

```python
import jax
import jax.numpy as jnp
from jax import lax
from jax.experimental import pallas as pl
from jax.experimental.pallas import tpu as pltpu
from jax.sharding import PartitionSpec as P

BF = jnp.bfloat16
F32 = jnp.float32
D, TOK, OWN, FFL, HD, Q = 4096, 512, 64, 1024, 256, 256
NCH, CW = 8, 512
TH = TOK // 2
NQ = 2 * NCH
HALF, QTR = OWN // 2, OWN // 4
WCH, WR = 4, 128
ARRIVAL = (0, 2, 3, 6, 1, 4, 5, 7)
LE, LI, LW = 5, 7, 5
S2, S3 = 1, 3
W0 = 7

NN = (((1,), (0,)), ((), ()))
NT = (((1,), (1,)), ((), ()))
TN = (((0,), (0,)), ((), ()))


def dot(a, b, dims=NN):
    return lax.dot_general(a, b, dims, preferred_element_type=F32)


class Place:
    def __init__(self):
        dp, tn = lax.axis_index("dp"), lax.axis_index("tensor")
        self.dp, self.tn = dp, tn
        self.x, self.h, self.c = dp // 4, (dp // 2) % 2, dp % 2
        self.z, self.l = tn // 2, tn % 2
        self.xu, self.xd, self.x2 = (self.x + 1) % 4, (self.x + 3) % 4, (self.x + 2) % 4
        self.zu, self.zd, self.z2 = (self.z + 1) % 4, (self.z + 3) % 4, (self.z + 2) % 4


def dp_of(x, h, c):
    return (x * 2 + h) * 2 + c


def tn_of(z, l):
    return z * 2 + l


def remote(src, dst, ss, rs, dev):
    return pltpu.make_async_remote_copy(
        src_ref=src, dst_ref=dst, send_sem=ss, recv_sem=rs, device_id=dev,
        device_id_type=pl.DeviceIdType.MESH,
    )


class TensorGather:
    def __init__(self, p, buf, ss, rs):
        z, l, zu, zd, z2, m = p.z, p.l, p.zu, p.zd, p.z2, 1 - p.l
        up, dn, pair = {"tensor": tn_of(zu, l)}, {"tensor": tn_of(zd, l)}, {"tensor": tn_of(z, m)}
        self.buf, self.ss, self.rs = buf, ss, rs
        self.t = [
            ((z, l), (z, m), 0, 64, pair),
            ((z, l), (zd, l), 0, 64, up),
            ((z, l), (zu, l), 0, 64, dn),
            ((z, m), (zd, m), 0, 64, up),
            ((z, m), (zu, m), 0, 64, dn),
            ((zd, l), (z2, l), 0, 32, up),
            ((zu, l), (z2, l), 32, 32, dn),
            ((zd, m), (z2, m), 0, 32, up),
            ((zu, m), (z2, m), 32, 32, dn),
        ]

    def _copy(self, i, received):
        sent, got, first, n, to = self.t[i]
        at = tn_of(*(got if received else sent)) * OWN + first
        ref = self.buf.at[pl.ds(pl.multiple_of(at, 16), n)]
        return remote(ref, ref, self.ss, self.rs.at[i], to)

    def send(self, *idx):
        for i in idx:
            self._copy(i, False).start()

    def recv(self, *idx):
        for i in idx:
            self._copy(i, True).wait_recv()

    def s0(self):
        self.send(1, 2, 0)

    def s1(self):
        self.recv(0)
        self.send(3, 4)

    def s2(self):
        self.recv(1)
        self.send(5)
        self.recv(2)
        self.send(6)

    def s3(self):
        self.recv(3)
        self.send(7)
        self.recv(4)
        self.send(8)

    def s4(self):
        self.recv(5, 6, 7, 8)

    def drain(self):
        sent = self.buf.at[pl.ds(0, 448)]
        remote(sent, sent, self.ss, self.rs.at[0], self.t[0][4]).wait_send()


class ColumnGather:
    def __init__(self, p, buf, base, ss, rs, up, dn, mate_a, mate_b):
        z, zu, zd, z2 = p.z, p.zu, p.zd, p.z2
        self.buf, self.base, self.ss, self.rs = buf, base, ss, rs
        a, b = (4, mate_a), (6, mate_b)
        self.t = [
            (z, 0, zd, up), (z, 1, zu, dn), (z, 1, zd, up), (z, 0, zu, dn),
            (z, 0, z, a), (z, 1, z, b),
            (zd, 0, z2, up), (zd, 0, zd, a),
            (zu, 1, z2, dn), (zu, 1, zu, b),
            (zd, 1, zd, b), (zu, 0, zu, a),
            (z2, 0, z2, a), (z2, 1, z2, b),
        ]

    def _rows(self, first):
        return self.buf.at[pl.ds(pl.multiple_of(self.base + first, 16), QTR)]

    def _copy(self, i, received):
        sent, half, got, to = self.t[i]
        if isinstance(to, tuple):
            base, dev = to
            dst = self._rows(base * HALF + got * QTR)
            src = dst if received else self._rows(sent * HALF + half * QTR)
        else:
            dev = to
            dst = self._rows((got if received else sent) * HALF + half * QTR)
            src = dst
        return remote(src, dst, self.ss, self.rs.at[i], dev)

    def send(self, *idx):
        for i in idx:
            self._copy(i, False).start()

    def recv(self, *idx):
        for i in idx:
            self._copy(i, True).wait_recv()

    def s0(self):
        self.send(0, 1, 2, 3, 4, 5)

    def s1(self):
        self.recv(0)
        self.send(6, 7)
        self.recv(1)
        self.send(8, 9)

    def s2(self):
        self.recv(2)
        self.send(10)
        self.recv(3)
        self.send(11)

    def s3(self):
        self.recv(6)
        self.send(12)
        self.recv(8)
        self.send(13)

    def s4(self):
        self.recv(4, 5, 7, 9, 10, 11, 12, 13)

    def drain(self):
        sent = self.buf.at[pl.ds(0, 14 * QTR)]
        remote(sent, sent, self.ss, self.rs.at[0], self.t[0][3]).wait_send()


class DpGather:
    def __init__(self, p, buf, ss, rs, rows):
        x, h, c, xu, xd, x2, o, g = p.x, p.h, p.c, p.xu, p.xd, p.x2, 1 - p.h, 1 - p.c
        up, dn = {"dp": dp_of(xu, h, c)}, {"dp": dp_of(xd, h, c)}
        pair, core = {"dp": dp_of(x, o, c)}, {"dp": dp_of(x, h, g)}
        self.buf, self.ss, self.rs = buf, ss, rs
        r, hf = rows, rows // 2
        self.t = [
            ((x, h, c), (x, h, g), 0, r, core),
            ((x, h, c), (x, o, c), 0, r, pair),
            ((x, h, c), (xd, h, c), 0, r, up),
            ((x, h, c), (xu, h, c), 0, r, dn),
            ((x, o, c), (xd, o, c), 0, r, up),
            ((x, o, c), (xu, o, c), 0, r, dn),
            ((xd, h, c), (x2, h, c), 0, hf, up),
            ((xu, h, c), (x2, h, c), hf, hf, dn),
            ((xd, o, c), (x2, o, c), 0, hf, up),
            ((xu, o, c), (x2, o, c), hf, hf, dn),
            ((x, o, c), (x, o, g), 0, r, core),
            ((xd, h, c), (xd, h, g), 0, r, core),
            ((xu, h, c), (xu, h, g), 0, r, core),
            ((xd, o, c), (xd, o, g), 0, r, core),
            ((xu, o, c), (xu, o, g), 0, r, core),
            ((x2, h, c), (x2, h, g), 0, r, core),
            ((x2, o, c), (x2, o, g), 0, r, core),
        ]

    def _copy(self, i, received):
        sent, got, first, n, to = self.t[i]
        sx, sh, sc = got if received else sent
        ref = self.buf.at[sc, sx * 2 + sh, pl.ds(first, n)]
        return remote(ref, ref, self.ss.at[i // 10], self.rs.at[i], to)

    def send(self, *idx):
        for i in idx:
            self._copy(i, False).start()

    def recv(self, *idx):
        for i in idx:
            self._copy(i, True).wait_recv()

    def s0(self):
        self.send(1, 2, 3, 0)

    def fwd(self, *ks):
        for k in ks:
            if k < 6:
                self.recv(k)
                if k == 1:
                    self.send(4, 5, 10)
                else:
                    self.send(k + 4, k + 9)
            elif k == 6:
                self.recv(6, 7)
                self.send(15)
            else:
                self.recv(8, 9)
                self.send(16)

    def done(self, *ks):
        for k in ks:
            self.recv(k + 9 if k else 0)

    def drain(self):
        for i, n in enumerate((8, 7)):
            sent = self.buf.at[0, pl.ds(0, n)]
            remote(sent, sent, self.ss.at[i], self.rs.at[0], self.t[0][4]).wait_send()


class RingReduce:
    def __init__(self, part, far, near, ysend, yrecv, ss, rs, ring, pair, up, dn, mate):
        self.part, self.far, self.near, self.ysend, self.yrecv = part, far, near, ysend, yrecv
        self.ss, self.rs = ss, rs
        self.r, self.ru, self.rd, self.r2 = ring
        self.l, self.m = pair, 1 - pair
        self.up, self.dn, self.mate = up, dn, mate

    def _copy(self, i, k):
        p = self.part(k)
        src, dst, to = [
            (lambda: p.at[self.r2 * 2], lambda: self.far.at[k, 0], self.up),
            (lambda: p.at[self.r2 * 2 + 1], lambda: self.far.at[k, 1], self.dn),
            (lambda: p.at[self.ru * 2 + 1], lambda: self.near.at[k, 1], self.up),
            (lambda: p.at[self.rd * 2], lambda: self.near.at[k, 2], self.dn),
            (lambda: p.at[self.ru * 2], lambda: self.near.at[k, 0], self.up),
            (lambda: p.at[self.rd * 2 + 1], lambda: self.near.at[k, 3], self.dn),
            (lambda: self.ysend.at[k], lambda: self.yrecv.at[k], self.mate),
        ][i]
        return remote(src(), dst(), self.ss.at[i], self.rs.at[k, (0, 1, 2, 2, 2, 2, 3)[i]], to)

    def stage1(self, k):
        for i in range(4):
            self._copy(i, k).start()

    def stage2(self, k):
        p = self.part(k)
        for i, blk in ((0, self.ru * 2), (1, self.rd * 2 + 1)):
            self._copy(i, k).wait_recv()
            p[blk] = (p[blk].astype(F32) + self.far[k, i].astype(F32)).astype(BF)
            self._copy(4 + i, k).start()

    def stage3(self, k):
        near = self.near.at[k]
        remote(near, near, self.ss.at[2], self.rs.at[k, 2], self.up).wait_recv()
        p = self.part(k)

        def total(pair):
            return (
                p[self.r * 2 + pair].astype(F32)
                + self.near[k, pair].astype(F32)
                + self.near[k, 2 + pair].astype(F32)
            )

        self.ysend[k] = total(self.m).astype(BF)
        self._copy(6, k).start()
        return total(self.l)

    def stage4(self, k):
        self._copy(6, k).wait_recv()
        return self.yrecv[k].astype(F32)

    def drain(self):
        for i in range(7):
            remote(self.ysend, self.ysend, self.ss.at[i], self.rs.at[0, 3], self.up).wait_send()


class ColumnReduce:
    def __init__(self, p, part, near, far, side, ss, rs, up, dn, mate_a, mate_b):
        self.z, self.zu, self.zd, self.z2 = p.z, p.zu, p.zd, p.z2
        self.part, self.near, self.far, self.side = part, near, far, side
        self.ss, self.rs = ss, rs
        self.up, self.dn, self.a, self.b = up, dn, mate_a, mate_b

    def _copy(self, i, k):
        lo, hi = pl.ds(0, QTR), pl.ds(QTR, QTR)
        src, dst, to = [
            (lambda: self.part.at[k, pl.ds(4, 2)], lambda: self.side.at[k, pl.ds(0, 2)], self.a),
            (lambda: self.part.at[k, pl.ds(6, 2)], lambda: self.side.at[k, pl.ds(2, 2)], self.b),
            (lambda: self.part.at[k, self.z2, lo], lambda: self.far.at[k, 0, lo], self.up),
            (lambda: self.part.at[k, self.z2, hi], lambda: self.far.at[k, 1, lo], self.dn),
            (lambda: self.part.at[k, self.zu, hi], lambda: self.near.at[k, 0, hi], self.up),
            (lambda: self.part.at[k, self.zd, lo], lambda: self.near.at[k, 1, lo], self.dn),
            (lambda: self.part.at[k, self.zu, lo], lambda: self.near.at[k, 0, lo], self.up),
            (lambda: self.part.at[k, self.zd, hi], lambda: self.near.at[k, 1, hi], self.dn),
        ][i]
        return remote(src(), dst(), self.ss.at[i], self.rs.at[k, (0, 0, 1, 2, 3, 3, 3, 3)[i]], to)

    def stage1(self, k):
        self._copy(0, k).start()
        self._copy(1, k).start()

    def stage2(self, k):
        side = self.side.at[k]
        remote(side, side, self.ss.at[0], self.rs.at[k, 0], self.a).wait_recv()
        for i in range(2):
            rows = pl.ds(QTR * i, QTR)
            for zz in range(4):
                got = self.side[k, 2 * i + zz // 2, pl.ds(QTR * (zz % 2), QTR)]
                self.part[k, zz, rows] = (
                    self.part[k, zz, rows].astype(F32) + got.astype(F32)
                ).astype(BF)
        for i in range(2, 6):
            self._copy(i, k).start()

    def stage3(self, k):
        for i, blk in ((0, self.zu), (1, self.zd)):
            self._copy(2 + i, k).wait_recv()
            rows = pl.ds(QTR * i, QTR)
            self.part[k, blk, rows] = (
                self.part[k, blk, rows].astype(F32) + self.far[k, i, pl.ds(0, QTR)].astype(F32)
            ).astype(BF)
            self._copy(6 + i, k).start()

    def stage4(self, k):
        near = self.near.at[k]
        remote(near, near, self.ss.at[4], self.rs.at[k, 3], self.up).wait_recv()
        return (
            self.part[k, self.z].astype(F32)
            + self.near[k, 0].astype(F32)
            + self.near[k, 1].astype(F32)
        )

    def drain(self):
        for i in range(8):
            sent = self.side.at[:, pl.ds(0, 2)] if i < 2 else self.far.at[:, 0, pl.ds(0, QTR)]
            remote(sent, sent, self.ss.at[i], self.rs.at[0, 3], self.up).wait_send()


def kernel(
    stream, final_gain, residual, ffn_gain, queries, keys, values, ctx, key_w, value_w,
    gate_hbm, up_hbm, down_hbm,
    out_ref, qg_ref, kwg_ref, vwg_ref, down_all,
    res_g, str_g, ffn_g, kvw, gate_v, up_v, down_v, part, far, near, ysend, yrecv,
    inear, coef_a, coef_b, ggrad, ugrad, acc, sgrad, kvg, kvg_t,
    crecv, wfar, wnear, wysend, wyrecv, wacc,
    res_ss, res_rs, str_ss, str_rs, ffn_ss, ffn_rs, kv_ss, kv_rs, dn_ss, dn_rs,
    er_ss, er_rs, ir_ss, ir_rs, wr_ss, wr_rs, cs_ss, cs_rs, loc, dsem,
):
    p = Place()
    MESH = pl.DeviceIdType.MESH
    z_up, z_dn = {"tensor": tn_of(p.zu, p.l)}, {"tensor": tn_of(p.zd, p.l)}
    mate = {"tensor": tn_of(p.z, 1 - p.l)}
    x_up, x_dn = {"dp": dp_of(p.xu, p.h, p.c)}, {"dp": dp_of(p.xd, p.h, p.c)}
    mate_b = {"dp": dp_of(p.x, 1 - p.h, p.c), "tensor": tn_of(p.z, 1 - p.l)}
    h_mate, core = {"dp": dp_of(p.x, 1 - p.h, p.c)}, {"dp": dp_of(p.x, p.h, 1 - p.c)}

    barrier = pltpu.get_barrier_semaphore()
    for dev in (z_up, z_dn, mate, mate_b, x_up, x_dn, h_mate, core):
        pl.semaphore_signal(barrier, inc=1, device_id=dev, device_id_type=MESH)

    own_chip = p.x * 2 + p.h
    gate_load = pltpu.make_async_copy(gate_hbm, gate_v, loc.at[0])
    up_load = pltpu.make_async_copy(up_hbm, up_v, loc.at[1])
    down_in = pltpu.make_async_copy(down_hbm, crecv.at[0], loc.at[2])
    down_in.start()
    down_own = pltpu.make_async_copy(crecv.at[0], down_all.at[p.c, own_chip], loc.at[3])
    gate_load.start()
    up_load.start()

    kvw[p.c, own_chip, 0:HD, :] = key_w[...]
    kvw[p.c, own_chip, HD : 2 * HD, :] = value_w[...]
    own = pl.multiple_of(p.tn * OWN, OWN)

    def normed(src, gain, dst, at):
        def body(i, _):
            r = pl.multiple_of(i * 16, 16)
            v = src[pl.ds(r, 16), :].astype(F32)
            s = lax.rsqrt(jnp.mean(v * v, axis=-1, keepdims=True) + 1e-06)
            dst[pl.ds(pl.multiple_of(at(i), 16), 16), :] = (v * s * gain[...]).astype(BF)
            return 0

        lax.fori_loop(0, OWN // 16, body, 0)

    kv = DpGather(p, kvw, kv_ss, kv_rs, 2 * HD)
    down = DpGather(p, down_all, dn_ss, dn_rs, FFL // WR)
    def column_gather(buf, ss, rs):
        return [
            ColumnGather(p, buf, b * TH, ss.at[b], rs.at[b], z_up, z_dn, mate, mate_b)
            for b in range(2)
        ]

    res = column_gather(res_g, res_ss, res_rs)
    stm = TensorGather(p, str_g, str_ss, str_rs)
    ffn = column_gather(ffn_g, ffn_ss, ffn_rs)

    pl.semaphore_wait(barrier, 8)
    kv.s0()
    normed(residual, ffn_gain, res_g, lambda i: (i // 2) * TH + p.z * HALF + (i % 2) * 16)
    res[0].s0()
    res[1].s0()
    normed(stream, final_gain, str_g, lambda i: own + i * 16)
    stm.s0()

    s_t = dot(keys[...], queries[...], NT)
    e_t = jnp.exp(s_t - jnp.max(s_t, axis=0, keepdims=True))
    probs = e_t / jnp.sum(e_t, axis=0, keepdims=True)
    pg = dot(values[...], ctx[...], NT)
    delta = jnp.sum(probs * pg, axis=0, keepdims=True)
    sg = (probs * (pg - delta)).astype(BF)
    vgrad = dot(probs.astype(BF), ctx[...])
    kgrad = dot(sg, queries[...])
    kvg[:, 0:HD] = kgrad.astype(BF)
    kvg[:, HD : 2 * HD] = vgrad.astype(BF)
    kvg_t[0:HD, :] = kgrad.T.astype(BF)
    kvg_t[HD : 2 * HD, :] = vgrad.T.astype(BF)
    qg_ref[...] = dot(sg, keys[...], TN).astype(BF)

    down_in.wait()
    down_own.start()

    ring_z = (p.z, p.zu, p.zd, p.z2)
    ring_x = (p.x, p.xu, p.xd, p.x2)
    enc_rs = RingReduce(
        lambda k: part.at[k], far, near, ysend, yrecv, er_ss, er_rs, ring_z, p.l, z_up, z_dn, mate
    )
    in_rs = ColumnReduce(
        p, part, inear, far, near, ir_ss, ir_rs, z_up, z_dn, mate, mate_b
    )
    w_rs = RingReduce(
        lambda k: kvw.at[p.c, :, pl.ds(pl.multiple_of(k * WR, WR), WR), :],
        wfar, wnear, wysend, wyrecv, wr_ss, wr_rs, ring_x, p.h, x_up, x_dn, h_mate,
    )

    def chunk_of(k):
        return [
            p.x * 2 + p.h, p.x * 2 + 1 - p.h, p.xd * 2 + p.h, p.xu * 2 + p.h,
            p.xd * 2 + 1 - p.h, p.xu * 2 + 1 - p.h, p.x2 * 2 + p.h, p.x2 * 2 + 1 - p.h,
        ][ARRIVAL[k]]

    def start_down():
        down_own.wait()
        down.s0()

    def enc_compute(k):
        chip = chunk_of(k)
        for cc in range(2):
            blk = dot(kvg[:, 0:HD], kvw[cc, chip, 0:HD, :], NT)
            blk = blk + dot(kvg[:, HD : 2 * HD], kvw[cc, chip, HD : 2 * HD, :], NT)
            blk = blk.astype(BF).reshape(8, 2, HALF, HD)
            for b in range(2):
                part[b * NCH + k, :, :, cc * HD : (cc + 1) * HD] = blk[:, b]

    def cols(k):
        return pl.ds(pl.multiple_of(chunk_of(k) * CW, CW), CW)

    def stream_back(b):
        rows = slice(b * HALF, (b + 1) * HALF)
        sq = jnp.zeros((HALF, 1), F32)
        ip = jnp.zeros((HALF, 1), F32)
        for k in range(NCH):
            v = stream[rows, cols(k)].astype(F32)
            sq = sq + jnp.sum(v * v, axis=-1, keepdims=True)
            ip = ip + jnp.sum(
                acc[b * NCH + k] * final_gain[:, cols(k)] * v, axis=-1, keepdims=True
            )
        scale = lax.rsqrt(sq * (1.0 / D) + 1e-06)
        mix = scale * scale * scale * (ip * (1.0 / D))
        at = pl.ds(pl.multiple_of(b * TH + p.z * HALF, HALF), HALF)
        for k in range(NCH):
            v = stream[rows, cols(k)].astype(F32)
            grad = scale * (acc[b * NCH + k] * final_gain[:, cols(k)]) - v * mix
            sgrad[rows, cols(k)] = grad
            ffn_g[at, cols(k)] = grad.astype(BF)
        ffn[b].s0()

    lag = LE
    F0 = NCH - 1 + 3 * lag
    before = {
        1: lambda: kv.fwd(2, 3),
        3: lambda: kv.fwd(6),
        4: lambda: kv.fwd(1),
        5: lambda: kv.fwd(4, 5),
        7: lambda: kv.fwd(7),
    }
    after = [
        (2, res[0].s1), (3, res[1].s1), (5, start_down), (6, res[0].s2), (7, res[1].s2),
        (8, res[0].s3), (9, res[1].s3), (11, lambda: down.fwd(2, 3)), (12, lambda: down.fwd(1)),
        (F0 + 3, ffn[0].s1), (F0 + 4, lambda: down.fwd(4, 5)), (F0 + 5, ffn[0].s2),
        (F0 + 6, ffn[0].s3), (F0 + 7, lambda: down.fwd(6, 7)),
    ]

    def flush(k):
        while after and after[0][0] <= k:
            after.pop(0)[1]()

    for k in range(NQ + 3 * lag):
        if k in before:
            before[k]()
        if k < NCH:
            kv.done(ARRIVAL[k])
            enc_compute(k)
        if k < NQ:
            enc_rs.stage1(k)
        flush(k)
        if 0 <= k - lag < NQ:
            enc_rs.stage2(k - lag)
        if 0 <= k - 2 * lag < NQ:
            acc[k - 2 * lag] = enc_rs.stage3(k - 2 * lag)
        if 0 <= k - 3 * lag < NQ:
            acc[k - 3 * lag] = acc[k - 3 * lag] + enc_rs.stage4(k - 3 * lag)
        if k - 3 * lag == NCH - 1:
            stream_back(0)
    stream_back(1)

    gate_load.wait()
    up_load.wait()
    res[0].s4()
    res[1].s4()

    def gate_tile(j):
        c0 = pl.ds(pl.multiple_of(j * HD, HD), HD)
        gate = dot(res_g[...], gate_v[:, c0])
        up = dot(res_g[...], up_v[:, c0])
        sig = 1.0 / (1.0 + jnp.exp(-gate))
        coef_a[:, c0] = (up * sig * (1.0 + gate * (1.0 - sig))).astype(BF)
        coef_b[:, c0] = (gate * sig).astype(BF)

    def gate_tiles(lo, hi):
        lax.fori_loop(lo, hi, lambda j, _: (gate_tile(j), 0)[1], 0)

    gate_tiles(0, 1)
    flush(99)
    ffn[1].s1()
    gate_tiles(1, 2)
    ffn[1].s2()
    stm.s1()
    gate_tiles(2, 3)
    ffn[1].s3()
    gate_tiles(3, 4)
    down.done(*range(8))

    def w_tile(chip, _):
        for cc in range(2):
            c0 = pl.ds(pl.multiple_of((chip * 2 + cc) * HD, HD), HD)
            kvw[cc, chip] = dot(kvg_t[...], str_g[:, c0]).astype(BF)
        return 0

    def down_load(j):
        s = j % 2
        return pltpu.make_async_copy(
            down_all.at[:, :, pl.ds(j * 2, 2)], down_v.at[s], dsem.at[s]
        )

    down_load(0).start()

    def core_copy(k):
        rows = pl.ds(pl.multiple_of(k * WR, WR), WR)
        return remote(
            kvw.at[1 - p.c, :, rows, :], crecv.at[k], cs_ss, cs_rs.at[k], core
        )

    enc_rs.drain()
    kv.drain()
    ffn[0].s4()

    def hidden(b):
        rows = slice(b * TH, (b + 1) * TH)

        def tile(j, _):
            @pl.when(j < 3)
            def _():
                down_load(j + 1).start()

            down_load(j).wait()
            s = j % 2
            hid = jnp.zeros((TH, HD), F32)
            for i in range(16):
                hid = hid + dot(
                    ffn_g[rows, i * HD : (i + 1) * HD],
                    down_v[s, i % 2, i // 2].reshape(HD, HD), NT,
                )
            c0 = pl.ds(pl.multiple_of(j * HD, HD), HD)
            ggrad[rows, c0] = (hid * coef_a[rows, c0].astype(F32)).astype(BF)
            ugrad[rows, c0] = (hid * coef_b[rows, c0].astype(F32)).astype(BF)
            return 0

        lax.fori_loop(0, 4, tile, 0)

    hidden(0)
    down_load(0).start()

    def in_step(k, _):
        @pl.when(k == NCH)
        def _():
            ffn[1].s4()
            hidden(1)

        @pl.when(k < NQ)
        def _():
            rows = pl.ds(pl.multiple_of((k % NCH) * CW, CW), CW)
            toks = pl.ds(pl.multiple_of((k // NCH) * TH, TH), TH)
            blk = dot(ggrad[toks, :], gate_v[rows, :], NT) + dot(ugrad[toks, :], up_v[rows, :], NT)
            part[k] = blk.astype(BF).reshape(8, HALF, CW)
            in_rs.stage1(k)

        @pl.when(k == S2)
        def _():
            stm.s2()

        @pl.when(k == S3)
        def _():
            stm.s3()

        @pl.when(k == W0)
        def _():
            stm.s4()
            lax.fori_loop(0, 8, w_tile, 0)
            for i in range(WCH):
                core_copy(i).start()

        w = k - W0 - 1

        @pl.when((w >= 0) & (w < WCH))
        def _():
            core_copy(w).wait_recv()
            mine = w_rs.part(w)
            mine[...] = (mine[...].astype(F32) + crecv[w].astype(F32)).astype(BF)
            w_rs.stage1(w)

        @pl.when((k >= 1 * LI) & (k < NQ + 1 * LI))
        def _():
            in_rs.stage2(k - LI)

        @pl.when((w >= 1 * LW) & (w < WCH + 1 * LW))
        def _():
            w_rs.stage2(w - LW)

        @pl.when((k >= 2 * LI) & (k < NQ + 2 * LI))
        def _():
            in_rs.stage3(k - 2 * LI)

        @pl.when((w >= 2 * LW) & (w < WCH + 2 * LW))
        def _():
            wacc[w - 2 * LW] = w_rs.stage3(w - 2 * LW)

        @pl.when((k >= 3 * LI) & (k < NQ + 3 * LI))
        def _():
            acc[k - 3 * LI] = in_rs.stage4(k - 3 * LI)

        @pl.when((w >= 3 * LW) & (w < WCH + 3 * LW))
        def _():
            wacc[w - 3 * LW] = wacc[w - 3 * LW] + w_rs.stage4(w - 3 * LW)

        return 0

    lax.fori_loop(0, max(NQ + 3 * LI, W0 + 1 + WCH + 3 * LW), in_step, 0)

    for half in range(2):
        kwg_ref[:, half * WR : (half + 1) * WR] = wacc[half].T.astype(BF)
        vwg_ref[:, half * WR : (half + 1) * WR] = wacc[2 + half].T.astype(BF)

    for b in range(2):
        rows = slice(b * HALF, (b + 1) * HALF)
        sq = jnp.zeros((HALF, 1), F32)
        ip = jnp.zeros((HALF, 1), F32)
        for k in range(NCH):
            c0 = slice(k * CW, (k + 1) * CW)
            v = residual[rows, c0].astype(F32)
            sq = sq + jnp.sum(v * v, axis=-1, keepdims=True)
            ip = ip + jnp.sum(acc[b * NCH + k] * ffn_gain[:, c0] * v, axis=-1, keepdims=True)
        scale = lax.rsqrt(sq * (1.0 / D) + 1e-06)
        mix = scale * scale * scale * (ip * (1.0 / D))
        for k in range(NCH):
            c0 = slice(k * CW, (k + 1) * CW)
            v = residual[rows, c0].astype(F32)
            out_ref[rows, c0] = (
                sgrad[rows, c0] + scale * (acc[b * NCH + k] * ffn_gain[:, c0]) - v * mix
            ).astype(BF)

    for g in (*res, stm, *ffn, down):
        g.drain()
    in_rs.drain()
    w_rs.drain()
    remote(crecv, crecv, cs_ss, cs_rs.at[0], core).wait_send()


def place_results(*refs):
    for src, dst in zip(refs[:4], refs[4:]):
        dst[...] = src[...]


def local(
    stream, final_gain, residual, ffn_gain, queries, saved_keys, saved_values, context_grad,
    key_weight, value_weight, gate_weight, up_weight, down_weight,
):
    vm = pl.BlockSpec(memory_space=pltpu.VMEM)
    hbm = pl.BlockSpec(memory_space=pl.ANY)
    dma = pltpu.SemaphoreType.DMA
    sds = jax.ShapeDtypeStruct
    v = pltpu.VMEM
    outs = pl.pallas_call(
        kernel,
        out_shape=(
            sds((OWN, D), BF), sds((Q, HD), BF), sds((HD, HD), BF), sds((HD, HD), BF),
            sds((2, 8, FFL // WR, WR, HD), BF),
        ),
        in_specs=[vm] * 10 + [hbm] * 3,
        out_specs=(vm, vm, vm, vm, hbm),
        scratch_shapes=[
            v((TOK, D), BF), v((TOK, D), BF), v((TOK, D), BF),
            v((2, 8, 2 * HD, HD), BF),
            v((D, FFL), BF), v((D, FFL), BF),
            v((2, 2, 8, 2, WR, HD), BF),
            v((NQ, 8, HALF, CW), BF),
            v((NQ, 2, HALF, CW), BF), v((NQ, 4, HALF, CW), BF),
            v((NQ, HALF, CW), BF), v((NQ, HALF, CW), BF),
            v((NQ, 2, HALF, CW), BF),
            v((TOK, FFL), BF), v((TOK, FFL), BF), v((TOK, FFL), BF), v((TOK, FFL), BF),
            v((NQ, HALF, CW), F32), v((OWN, D), F32),
            v((TOK, 2 * HD), BF), v((2 * HD, TOK), BF),
            v((WCH, 8, WR, HD), BF),
            v((WCH, 2, WR, HD), BF), v((WCH, 4, WR, HD), BF),
            v((WCH, WR, HD), BF), v((WCH, WR, HD), BF), v((WCH, WR, HD), F32),
            dma((2,)), dma((2, 14)), dma, dma((9,)), dma((2,)), dma((2, 14)),
            dma((2,)), dma((17,)), dma((2,)), dma((17,)),
            dma((7,)), dma((NQ, 4)), dma((8,)), dma((NQ, 4)),
            dma((7,)), dma((WCH, 4)), dma, dma((WCH,)),
            dma((4,)), dma((2,)),
        ],
        compiler_params=pltpu.CompilerParams(
            collective_id=0, has_side_effects=True, vmem_limit_bytes=64 * 1024 * 1024
        ),
        name="cross_ffn_backward",
    )(
        stream, final_gain.reshape(1, D), residual, ffn_gain.reshape(1, D), queries, saved_keys,
        saved_values, context_grad, key_weight, value_weight, gate_weight, up_weight,
        down_weight.reshape(FFL // WR, WR, HD),
    )
    return pl.pallas_call(
        place_results,
        out_shape=tuple(sds(o.shape, o.dtype) for o in outs[:4]),
        in_specs=[vm] * 4,
        out_specs=(vm,) * 4,
        name="place_results",
    )(*outs[:4])


def solution(mesh):
    return jax.shard_map(
        local,
        mesh=mesh,
        in_specs=(
            P(("dp", "tensor"), None), P(), P(("dp", "tensor"), None), P(),
            P("dp", "tensor"), P("dp", "tensor"), P("dp", "tensor"), P("dp", "tensor"),
            P("dp", "tensor"), P("dp", "tensor"), P(None, "tensor"), P(None, "tensor"),
            P("tensor", "dp"),
        ),
        out_specs=(
            P(("dp", "tensor"), None), P("dp", "tensor"), P("dp", "tensor"), P("dp", "tensor"),
        ),
        check_vma=False,
    )
```
